32 devices in a mesh: dp: 16 (over z, x, core), mp: 2 (over y).
Axes of the slice: x: 2, y: 2, z: 4, core: 2. Of those that a mesh axis runs over, the one named last changes fastest.
Arguments:
- prompt_hidden: bfloat16 [8192, 5120], P('dp'), may hold values from -6 to 6
- w_key: bfloat16 [5120, 512], P(None, 'mp'), may hold values from -0.078125 to 0.078125
- w_value: bfloat16 [5120, 512], P(None, 'mp'), may hold values from -0.078125 to 0.078125
- queries: bfloat16 [8192, 4096], P('dp', 'mp'), may hold values from -170 to 170
- resp_key: bfloat16 [8192, 512], P('dp', 'mp'), may hold values from -6.1 to 6.1
- resp_value: bfloat16 [8192, 512], P('dp', 'mp'), may hold values from -6 to 6
- cotangent: bfloat16 [8192, 4096], P('dp', 'mp'), may hold values from -6 to 6
- group_offset: int32 [32], P('dp'), may hold values from 0 to 3, as said below
- resp_length: int32 [32], P('dp'), may hold values from 1 to 256
Outputs:
- attn_out: bfloat16 [8192, 4096], P('dp', 'mp')
- query_grad: bfloat16 [8192, 4096], P('dp', 'mp')
- resp_key_grad: bfloat16 [8192, 512], P('dp', 'mp')
- resp_value_grad: bfloat16 [8192, 512], P('dp', 'mp')
- hidden_grad: bfloat16 [8192, 5120], P('dp', 'mp')
- w_key_grad: float32 [5120, 512], P('dp', 'mp')
- w_value_grad: float32 [5120, 512], P('dp', 'mp')
The draws below stay inside these ranges and needn't reach their ends.
Inputs may be any that keep to these rules, and one draw needn't show every extreme that they name: `group_offset`: counted cyclically along dp.
All inputs are finite; a program needn't handle non-finite values.
Results may differ from the reference program's by a relative error of at most 0.0095.
Values may be sent and summed in bfloat16 or wider, within the bound.
No kernel may reach another device: no remote copies, remote signals or barrier semaphores. Data moves between devices by JAX's collectives and lax.ppermute only.
A program may use at most 256 MiB of HBM per device.

```python
import jax
import jax.numpy as jnp
from jax import lax

D = 5120
QH = 32
KVH = 4
HD = 128
PLEN = 512
RLEN = 256
RESP_DEV = 2
REACH = 4
PROMPT_ROWS = 8192
ROWS = 8192
N_DP = 16


def shared_keys(key):
    row_total = N_DP * RESP_DEV * RLEN
    return jnp.clip(jax.random.normal(key, (row_total, KVH * HD), jnp.float32), -6.0, 6.0)


def draw_resp_key(key, part):
    base_keys = shared_keys(key)
    return base_keys.astype(jnp.bfloat16)


def draw_queries(key, part):
    key = jax.random.fold_in(key, 5)
    row_total = N_DP * RESP_DEV * RLEN
    drawn_values = jnp.clip(jax.random.normal(key, (row_total, QH * HD), jnp.float32), -6.0, 6.0)
    return drawn_values.astype(jnp.bfloat16)


def draw_group_offset(key, part):
    key = jax.random.fold_in(key, 21)
    offsets = jax.random.randint(key, (N_DP * RESP_DEV,), 0, REACH, jnp.int32)
    offsets = offsets.at[0].set(REACH - 1)
    return offsets.at[1].set(0)


def draw_resp_length(key, part):
    key = jax.random.fold_in(key, 33)
    lengths = jax.random.randint(key, (N_DP * RESP_DEV,), 1, RLEN + 1, jnp.int32)
    return lengths.at[0].set(RLEN)


def raised(values, key, source, target, parts, factor):
    def block_of(dim):
        return (jnp.arange(values.shape[dim]) // (values.shape[dim] // parts)).reshape((-1,) + (1,) * (values.ndim - 1 - dim))

    one_side = jax.random.permutation(key, parts)[block_of(target)]
    other_side = (block_of(target) + parts // 2) % parts
    return jnp.where((block_of(source) == one_side) | (block_of(source) == other_side), factor * values, values)


def block_levels(key, shape, split, smallest, top_value):
    def one(dim, parts):
        steps = jax.random.uniform(jax.random.fold_in(jax.random.fold_in(key, 6), dim), (parts,), jnp.float32, smallest / len(split), top_value / len(split))
        return jnp.repeat(jnp.exp(steps), shape[dim] // parts).reshape((-1,) + (1,) * (len(shape) - dim - 1))

    loudness = one(*split[0])
    for cut in split[1:]:
        loudness = loudness * one(*cut)
    return loudness


def normal_values(rng, shape, spread, most, shards=(), held_as=jnp.bfloat16):
    loudness = block_levels(rng, shape, shards, -0.22, 0.18) if shards else 1.0
    entries = jax.random.normal(rng, shape, jnp.float32) * spread * loudness
    return jnp.minimum(jnp.maximum(entries, -most), most).astype(held_as)


def gaussian_with(key, dims, scale, bound, cuts, heavy, kind=jnp.bfloat16):
    array = scale * jax.random.normal(key, dims, jnp.float32)
    if cuts:
        array = array * block_levels(key, dims, cuts, -0.22, 0.18)
    return jnp.clip(raised(array, jax.random.fold_in(key, 3), *heavy), -bound, bound).astype(kind)


def setup_inputs(seed: int = 0) -> dict:
    splits = jax.random.split(jax.random.key(seed), 10)
    return {
        "prompt_hidden": gaussian_with(splits[0], (PROMPT_ROWS, D), 1.0, 6.0, ((0, 16),), (0, 1, 16, 2.0)),
        "w_key": normal_values(splits[1], (D, KVH * HD), D ** -0.5, 0.078125, ((1, 2),)),
        "w_value": normal_values(splits[2], (D, KVH * HD), D ** -0.5, 0.078125, ((1, 2),)),
        "queries": draw_queries(jax.random.fold_in(splits[9], 71), 0),
        "resp_key": draw_resp_key(jax.random.fold_in(splits[9], 71), 0),
        "resp_value": normal_values(splits[5], (ROWS, KVH * HD), 1.0, 6.0, ((0, 16), (1, 2))),
        "cotangent": normal_values(splits[6], (ROWS, QH * HD), 1.0, 6.0, ((0, 16), (1, 2))),
        "group_offset": draw_group_offset(jax.random.fold_in(splits[9], 71), 0),
        "resp_length": draw_resp_length(jax.random.fold_in(splits[9], 71), 0),
    }


def attend(query, key_rows, value_rows, length, dout):
    row_count = query.shape[0]
    heads_kv = key_rows.shape[1] // HD
    group_size = query.shape[1] // key_rows.shape[1]
    prompt_len = key_rows.shape[0] - row_count
    query_heads = query.astype(jnp.float32).reshape(row_count, heads_kv, group_size, HD)
    key_heads = key_rows.astype(jnp.float32).reshape(-1, heads_kv, HD)
    value_heads = value_rows.astype(jnp.float32).reshape(-1, heads_kv, HD)
    score_scale = HD ** -0.5
    scores = jnp.einsum("qgnd,kgd->gnqk", query_heads, key_heads) * score_scale
    position = jnp.arange(row_count, dtype=jnp.int32)
    key_position = jnp.arange(key_rows.shape[0], dtype=jnp.int32) - prompt_len
    allowed = key_position[None, :] <= position[:, None]
    scores = jnp.where(allowed, scores, -jnp.inf)
    peak_score = jnp.max(scores, axis=-1, keepdims=True)
    shifted = jnp.exp(scores - peak_score)
    probs = shifted / jnp.sum(shifted, axis=-1, keepdims=True)
    weights = probs.astype(jnp.bfloat16).astype(jnp.float32)
    live_rows = (position < length)[:, None, None, None]
    attended = jnp.einsum("gnqk,kgd->qgnd", weights, value_heads)
    attended = jnp.where(live_rows, attended, 0.0).reshape(row_count, -1).astype(jnp.bfloat16)
    grad_out = jnp.where(live_rows, dout.astype(jnp.float32).reshape(row_count, heads_kv, group_size, HD), 0.0)
    prob_grad = jnp.einsum("qgnd,kgd->gnqk", grad_out, value_heads)
    delta_sum = jnp.sum(probs * prob_grad, axis=-1, keepdims=True)
    score_grad = (probs * (prob_grad - delta_sum) * score_scale).astype(jnp.bfloat16).astype(jnp.float32)
    query_grad = jnp.einsum("gnqk,kgd->qgnd", score_grad, key_heads).reshape(row_count, -1).astype(jnp.bfloat16)
    key_grad = jnp.einsum("gnqk,qgnd->kgd", score_grad, query_heads).reshape(key_rows.shape[0], -1)
    value_grad = jnp.einsum("gnqk,qgnd->kgd", weights, grad_out).reshape(key_rows.shape[0], -1)
    return attended, query_grad, key_grad, value_grad


def reference(prompt_hidden, w_key, w_value, queries, resp_key, resp_value, cotangent, group_offset, resp_length):
    key_width = w_key.shape[1]
    prompt_key = jnp.dot(prompt_hidden, w_key, preferred_element_type=jnp.float32).astype(jnp.bfloat16).reshape(N_DP, PLEN, key_width)
    prompt_value = jnp.dot(prompt_hidden, w_value, preferred_element_type=jnp.float32).astype(jnp.bfloat16).reshape(N_DP, PLEN, key_width)
    resp_total = N_DP * RESP_DEV

    def respond(carried, inputs):
        key_sum, value_sum = carried
        query, own_key, own_value, dout, offset, length, resp_index = inputs
        owner_id = ((resp_index // RESP_DEV - offset) % N_DP).astype(jnp.int32)
        key_rows = jnp.concatenate([lax.dynamic_index_in_dim(prompt_key, owner_id, 0, keepdims=False), own_key], axis=0)
        value_rows = jnp.concatenate([lax.dynamic_index_in_dim(prompt_value, owner_id, 0, keepdims=False), own_value], axis=0)
        attended, query_grad, key_grad, value_grad = attend(query, key_rows, value_rows, length, dout)
        key_sum = key_sum.at[owner_id].add(key_grad[:PLEN])
        value_sum = value_sum.at[owner_id].add(value_grad[:PLEN])
        outputs = (attended, query_grad, key_grad[PLEN:].astype(jnp.bfloat16), value_grad[PLEN:].astype(jnp.bfloat16))
        return (key_sum, value_sum), outputs

    zeros = jnp.zeros((N_DP, PLEN, key_width), jnp.float32)
    inputs = (queries.reshape(resp_total, RLEN, -1), resp_key.reshape(resp_total, RLEN, -1),
              resp_value.reshape(resp_total, RLEN, -1), cotangent.reshape(resp_total, RLEN, -1),
              group_offset, resp_length, jnp.arange(resp_total, dtype=jnp.int32))
    (key_sum, value_sum), outputs = lax.scan(respond, (zeros, zeros), inputs)
    attn_out = outputs[0].reshape(ROWS, -1)
    query_grad = outputs[1].reshape(ROWS, -1)
    resp_key_grad = outputs[2].reshape(ROWS, -1)
    resp_value_grad = outputs[3].reshape(ROWS, -1)
    prompt_key_grad = key_sum.reshape(PROMPT_ROWS, key_width).astype(jnp.bfloat16)
    prompt_value_grad = value_sum.reshape(PROMPT_ROWS, key_width).astype(jnp.bfloat16)
    hidden_grad = (jnp.dot(prompt_key_grad, w_key.T, preferred_element_type=jnp.float32)
                   + jnp.dot(prompt_value_grad, w_value.T, preferred_element_type=jnp.float32)).astype(jnp.bfloat16)
    w_key_grad = jnp.dot(prompt_hidden.T, prompt_key_grad, preferred_element_type=jnp.float32)
    w_value_grad = jnp.dot(prompt_hidden.T, prompt_value_grad, preferred_element_type=jnp.float32)
    return (attn_out, query_grad, resp_key_grad, resp_value_grad, hidden_grad, w_key_grad, w_value_grad)
```

```python
import functools
import math

import jax
import jax.numpy as jnp
from jax import lax
from jax.experimental import pallas as pl
from jax.experimental.pallas import tpu as pltpu
from jax.sharding import PartitionSpec as P

HD = 128
REACH = 4
LOG2E = 1.4426950408889634
BF = jnp.bfloat16
F32 = jnp.float32
NT = (((1,), (1,)), ((), ()))
NN = (((1,), (0,)), ((), ()))
TN = (((0,), (0,)), ((), ()))
MIB = 1024 * 1024


def mm(a, b, dims=NN):
    return lax.dot_general(a, b, dims, preferred_element_type=F32)


def permute(block, axis, target):
    return lax.ppermute(block, axis, [(i, target(i)) for i in range(lax.axis_size(axis))])


def project_kernel(h_ref, wk_ref, wv_ref, *rest):
    *outs, acc = rest
    step = pl.program_id(0)
    width = wk_ref.shape[1]
    key = mm(h_ref[...], wk_ref[...])
    value = mm(h_ref[...], wv_ref[...])

    @pl.when(step == 0)
    def _():
        acc[:, :width] = key
        acc[:, width:] = value

    @pl.when(step > 0)
    def _():
        acc[:, :width] += key
        acc[:, width:] += value

    @pl.when(step == pl.num_programs(0) - 1)
    def _():
        for g, out in enumerate(outs):
            out[0] = acc[:, g * HD : (g + 1) * HD].astype(BF)
            out[1] = acc[:, width + g * HD : width + (g + 1) * HD].astype(BF)


def project(hidden, w_key, w_value):
    rows, depth = hidden.shape
    width = w_key.shape[1]
    tile = 512
    groups = width // HD
    return pl.pallas_call(
        project_kernel,
        out_shape=[jax.ShapeDtypeStruct((2, rows, HD), BF)] * groups,
        grid=(depth // tile,),
        in_specs=[
            pl.BlockSpec((rows, tile), lambda i: (0, i)),
            pl.BlockSpec((tile, width), lambda i: (i, 0)),
            pl.BlockSpec((tile, width), lambda i: (i, 0)),
        ],
        out_specs=[pl.BlockSpec((2, rows, HD), lambda i: (0, 0, 0))] * groups,
        scratch_shapes=[pltpu.VMEM((rows, 2 * width), F32)],
        compiler_params=pltpu.CompilerParams(vmem_limit_bytes=32 * MIB),
        cost_estimate=pl.CostEstimate(
            flops=4 * rows * depth * width,
            bytes_accessed=2 * depth * (rows + 2 * width),
            transcendentals=0,
        ),
        name="project",
    )(hidden, w_key, w_value)


def attend_kernel(heads, sel_ref, len_ref, q_ref, do_ref, *rest):
    kv_refs, (rk_ref, rv_ref), rest = rest[:REACH], rest[REACH : REACH + 2], rest[REACH + 2 :]
    (o_ref, dq_ref, rdk_ref, rdv_ref, part_ref, k_s, v_s, kt_s, vt_s, dk_s, dv_s, first_s) = rest[-12:]
    r = pl.program_id(0)
    plen = kv_refs[0].shape[1]
    rlen = q_ref.shape[0]
    sel = sel_ref[r]
    for j, ref in enumerate(kv_refs):

        @pl.when(sel == j)
        def _():
            k_s[:plen] = ref[0]
            v_s[:plen] = ref[1]

    k_s[plen:] = rk_ref[...]
    v_s[plen:] = rv_ref[...]
    kt_s[...] = k_s[...].T
    vt_s[...] = v_s[...].T
    scale = HD**-0.5
    c = scale * LOG2E
    live = lax.broadcasted_iota(jnp.int32, (1, rlen), 1) < len_ref[r]
    livef = live.astype(F32)
    key_pos = lax.broadcasted_iota(jnp.int32, (rlen, rlen), 0)
    allowed = key_pos <= lax.broadcasted_iota(jnp.int32, (rlen, rlen), 1)
    for h in range(heads):
        cols = pl.ds(h * HD, HD)
        q = q_ref[:, cols]
        s = mm(k_s[...], q, NT)
        sp = s[:plen]
        sr = jnp.where(allowed, s[plen:], -jnp.inf)
        m = jnp.maximum(jnp.max(sp, axis=0, keepdims=True), jnp.max(sr, axis=0, keepdims=True))
        e = jnp.concatenate([jnp.exp2((sp - m) * c), jnp.exp2((sr - m) * c)], axis=0)
        eb = e.astype(BF)
        inv = livef / jnp.sum(e, axis=0, keepdims=True)
        ot = mm(vt_s[...], eb) * inv
        o_ref[:, cols] = ot.T.astype(BF)
        dob = (do_ref[:, cols].T.astype(F32) * inv).astype(BF)
        delta = jnp.sum(dob.astype(F32) * ot, axis=0, keepdims=True)
        ds = (e * (mm(v_s[...], dob) - delta)).astype(BF)
        dq_ref[:, cols] = (mm(kt_s[...], ds) * scale).T.astype(BF)
        dv = mm(eb, dob, NT)
        dk = mm(ds, q)
        if h == 0:
            dk_s[...] = dk
            dv_s[...] = dv
        else:
            dk_s[...] += dk
            dv_s[...] += dv
    rdk_ref[...] = (dk_s[plen:] * scale).astype(BF)
    rdv_ref[...] = dv_s[plen:].astype(BF)

    @pl.when(r == 0)
    def _():
        first_s[0] = dk_s[:plen]
        first_s[1] = dv_s[:plen]

    @pl.when(r == 1)
    def _():
        one, two = sel_ref[0], sel_ref[1]
        for j in range(REACH):

            @pl.when((one != j) & (two != j))
            def _():
                part_ref[j] = jnp.zeros(part_ref.shape[1:], BF)

            @pl.when((one == j) & (two != j))
            def _():
                part_ref[j, 0] = (first_s[0] * scale).astype(BF)
                part_ref[j, 1] = first_s[1].astype(BF)

            @pl.when((one != j) & (two == j))
            def _():
                part_ref[j, 0] = (dk_s[:plen] * scale).astype(BF)
                part_ref[j, 1] = dv_s[:plen].astype(BF)

            @pl.when((one == j) & (two == j))
            def _():
                part_ref[j, 0] = ((first_s[0] + dk_s[:plen]) * scale).astype(BF)
                part_ref[j, 1] = (first_s[1] + dv_s[:plen]).astype(BF)


def attend(g, sel, lengths, q, dout, kvs, rk, rv, prev):
    rows, width = q.shape
    slots = sel.shape[0]
    rlen = rows // slots
    gw = width // (rk.shape[1] // HD)
    heads = gw // HD
    plen = kvs[0].shape[1]
    klen = plen + rlen
    wide = pl.BlockSpec((rlen, gw), lambda r, *_: (r, g))
    narrow = pl.BlockSpec((rlen, HD), lambda r, *_: (r, g))
    pair = pl.BlockSpec((2, plen, HD), lambda r, *_: (0, 0, 0))
    ins = [q, dout, *kvs, rk, rv]
    in_specs = [wide, wide] + [pair] * REACH + [narrow, narrow]
    aliases = {}
    if prev is not None:
        aliases = {2 + len(ins) + i: i for i in range(4)}
        ins += list(prev)
        in_specs += [pl.BlockSpec(memory_space=pl.ANY)] * 4
    return pl.pallas_call(
        functools.partial(attend_kernel, heads),
        out_shape=[jax.ShapeDtypeStruct(q.shape, BF)] * 2
        + [jax.ShapeDtypeStruct(rk.shape, BF)] * 2
        + [jax.ShapeDtypeStruct((REACH, 2, plen, HD), BF)],
        grid_spec=pltpu.PrefetchScalarGridSpec(
            num_scalar_prefetch=2,
            grid=(slots,),
            in_specs=in_specs,
            out_specs=[wide, wide, narrow, narrow]
            + [pl.BlockSpec((REACH, 2, plen, HD), lambda r, *_: (0, 0, 0, 0))],
            scratch_shapes=[pltpu.VMEM((klen, HD), BF)] * 2
            + [pltpu.VMEM((HD, klen), BF)] * 2
            + [pltpu.VMEM((klen, HD), F32)] * 2
            + [pltpu.VMEM((2, plen, HD), F32)],
        ),
        input_output_aliases=aliases,
        compiler_params=pltpu.CompilerParams(vmem_limit_bytes=40 * MIB),
        cost_estimate=pl.CostEstimate(
            flops=slots * heads * 24 * rlen * klen * HD,
            bytes_accessed=8 * MIB,
            transcendentals=slots * heads * rlen * klen,
        ),
        name=f"attend_{g}",
    )(sel, lengths, *ins)


def weight_kernel(side_ref, h_ref, grad_ref, keep_ref, send_ref, both):
    pairs, half = keep_ref.shape[:2]
    for j in range(2):
        both[:, j * HD : (j + 1) * HD] = mm(h_ref[...], grad_ref[j], TN).astype(BF)
    side = side_ref[0]
    for p in range(pairs):
        keep_ref[p] = both[pl.ds(pl.multiple_of((2 * p + side) * half, half), half), :]
        send_ref[p] = both[pl.ds(pl.multiple_of((2 * p + 1 - side) * half, half), half), :]


def weight_terms(side, hidden, grad, parts):
    rows, depth = hidden.shape
    chunk = depth // parts
    pairs = HD // math.gcd(2 * chunk, HD)
    tile = 2 * chunk * pairs
    out = jax.ShapeDtypeStruct((parts // 2, chunk, 2 * HD), BF)
    spec = pl.BlockSpec((pairs, chunk, 2 * HD), lambda i, *_: (i, 0, 0))
    return pl.pallas_call(
        weight_kernel,
        out_shape=[out, out],
        grid_spec=pltpu.PrefetchScalarGridSpec(
            num_scalar_prefetch=1,
            grid=(depth // tile,),
            in_specs=[
                pl.BlockSpec((rows, tile), lambda i, *_: (0, i)),
                pl.BlockSpec((2, rows, HD), lambda i, *_: (0, 0, 0)),
            ],
            out_specs=[spec, spec],
            scratch_shapes=[pltpu.VMEM((tile, 2 * HD), BF)],
        ),
        compiler_params=pltpu.CompilerParams(vmem_limit_bytes=32 * MIB),
        cost_estimate=pl.CostEstimate(
            flops=4 * rows * depth * HD,
            bytes_accessed=2 * depth * (rows + 2 * HD),
            transcendentals=0,
        ),
        name="weight_terms",
    )(side, hidden, grad)


def halve(keep, send, index, size):
    count = keep.shape[0]
    bit = 1
    held = keep.astype(F32) + permute(send, "dp", lambda i: i ^ 1).astype(F32)
    while count > 1:
        bit *= 2
        mine = (index // bit) % 2
        split = held.reshape(count // 2, 2, *held.shape[1:])
        out = lax.dynamic_index_in_dim(split, 1 - mine, 1, keepdims=False).astype(BF)
        stay = lax.dynamic_index_in_dim(split, mine, 1, keepdims=False)
        held = stay + permute(out, "dp", lambda i: i ^ bit).astype(F32)
        count //= 2
    return held[0]


def hidden_kernel(half_ref, own_ref, far_ref, wk_ref, wv_ref, wa_ref, wb_ref, out_ref):
    total = mm(own_ref[0], wk_ref[...], NT) + mm(own_ref[1], wv_ref[...], NT)
    total += mm(far_ref[0], wa_ref[...], NT) + mm(far_ref[1], wb_ref[...], NT)
    out_ref[...] = total.astype(BF)


def hidden_grads(half, own, far, w_key, w_value, far_a, far_b):
    rows, width = own.shape[1:]
    cols = far_a.shape[0]
    tile = 512
    whole = pl.BlockSpec((2, rows, width), lambda i, *_: (0, 0, 0))
    near = pl.BlockSpec((tile, width), lambda i, half: (half[0] * (cols // tile) + i, 0))
    away = pl.BlockSpec((tile, width), lambda i, *_: (i, 0))
    return pl.pallas_call(
        hidden_kernel,
        out_shape=jax.ShapeDtypeStruct((rows, cols), BF),
        grid_spec=pltpu.PrefetchScalarGridSpec(
            num_scalar_prefetch=1,
            grid=(cols // tile,),
            in_specs=[whole, whole, near, near, away, away],
            out_specs=pl.BlockSpec((rows, tile), lambda i, *_: (0, i)),
        ),
        compiler_params=pltpu.CompilerParams(vmem_limit_bytes=32 * MIB),
        cost_estimate=pl.CostEstimate(
            flops=8 * rows * cols * width,
            bytes_accessed=2 * cols * (rows + 4 * width),
            transcendentals=0,
        ),
        name="hidden_grads",
    )(half, own, far, w_key, w_value, far_a, far_b)


def body(
    prompt_hidden,
    w_key,
    w_value,
    queries,
    resp_key,
    resp_value,
    cotangent,
    group_offset,
    resp_length,
):
    size = lax.axis_size("dp")
    index = lax.axis_index("dp")
    core = index % 2
    half = lax.axis_index("mp")
    groups = w_key.shape[1] // HD
    cols = w_key.shape[0] // 2

    mine = jnp.where(
        core == 0,
        lax.dynamic_slice_in_dim(w_key, (1 - half) * cols, cols, 0),
        lax.dynamic_slice_in_dim(w_value, (1 - half) * cols, cols, 0),
    )
    far_a = permute(mine, "mp", lambda i: 1 - i)
    far_b = permute(far_a, "dp", lambda i: i ^ 1)

    def other(i):
        return (i + 1) % size if i % 2 == 0 else (i + 3) % size

    def back(i):
        return (i - 1) % size if i % 2 == 1 else (i - 3) % size

    sel = jnp.where((group_offset % 2 == 1) & (core == 0), 4 - group_offset, group_offset)

    pairs = project(prompt_hidden, w_key, w_value)
    received = []
    for pair in pairs:
        two = permute(pair, "dp", lambda i: (i + 2) % size)
        one = permute(pair, "dp", other)
        three = permute(two, "dp", lambda i: i ^ 1)
        received.append([pair, one, two, three])

    prev = None
    owns = []
    fars = []
    terms = []
    for g in range(groups):
        *prev, part = attend(
            g, sel, resp_length, queries, cotangent, received[g], resp_key, resp_value, prev
        )
        swapped = permute(part[3], "dp", lambda i: i ^ 1)
        from_other = permute(part[1], "dp", back)
        two = (part[2].astype(F32) + swapped.astype(F32)).astype(BF)
        from_two = permute(two, "dp", lambda i: (i - 2) % size)
        grad = (part[0].astype(F32) + from_other.astype(F32) + from_two.astype(F32)).astype(BF)
        owns.append(grad)
        fars.append(permute(grad, "mp", lambda i: 1 - i))
        keep, send = weight_terms(core.reshape(1), prompt_hidden, grad, size)
        terms.append(halve(keep, send, index, size))
    own = jnp.concatenate(owns, axis=-1)
    far = jnp.concatenate(fars, axis=-1)
    far = jnp.where(core == 0, far, far[::-1])
    hidden_grad = hidden_grads(half.reshape(1), own, far, w_key, w_value, far_a, far_b)
    return (
        *prev,
        hidden_grad,
        jnp.concatenate([t[:, :HD] for t in terms], axis=-1),
        jnp.concatenate([t[:, HD:] for t in terms], axis=-1),
    )


def solution(mesh):
    placed = (
        P("dp", None),
        P(None, "mp"),
        P(None, "mp"),
        P("dp", "mp"),
        P("dp", "mp"),
        P("dp", "mp"),
        P("dp", "mp"),
        P("dp"),
        P("dp"),
    )
    return jax.shard_map(
        body,
        mesh=mesh,
        in_specs=placed,
        out_specs=(P("dp", "mp"),) * 7,
        check_vma=False,
    )
```

```python
import functools
import math

import jax
import jax.numpy as jnp
from jax import lax
from jax.experimental import pallas as pl
from jax.experimental.pallas import tpu as pltpu
from jax.sharding import PartitionSpec as P

HD = 128
REACH = 4
ONES = 16
LOG2E = 1.4426950408889634
BF = jnp.bfloat16
F32 = jnp.float32
NT = (((1,), (1,)), ((), ()))
NN = (((1,), (0,)), ((), ()))
TN = (((0,), (0,)), ((), ()))
MIB = 1024 * 1024
VMEM = 32 * MIB
WHOLE = 58 * MIB
RESIDENT = pl.BlockSpec(memory_space=pltpu.VMEM)


def mm(a, b, dims=NN):
    return lax.dot_general(a, b, dims, preferred_element_type=F32)


def permute(block, axis, target, name):
    with jax.named_scope(name):
        return lax.ppermute(block, axis, [(i, target(i)) for i in range(lax.axis_size(axis))])


def after(values, *others):
    return lax.optimization_barrier((values, others))[0]


def project_kernel(groups, at_ref, h_ref, wk_ref, wv_ref, *rest):
    outs, (keep_ref, send_ref, mine_ref), rest = rest[:groups], rest[groups : groups + 3], rest[groups + 3 :]
    h_s, wk_s, wv_s, turned, in_sems, out_sems, mine_sems = rest
    steps, rows, tile = h_s.shape
    width = wk_s.shape[2]
    chunk = keep_ref.shape[1]
    pairs = tile // (2 * chunk)
    half, core = at_ref[0], at_ref[1]
    copies = []
    for j in range(steps):
        at = pl.ds(j * tile, tile)
        copies.append(
            [
                pltpu.make_async_copy(h_ref.at[:, at], h_s.at[j], in_sems.at[j, 0]),
                pltpu.make_async_copy(wk_ref.at[at], wk_s.at[j], in_sems.at[j, 1]),
                pltpu.make_async_copy(wv_ref.at[at], wv_s.at[j], in_sems.at[j, 2]),
            ]
        )
        for copy in copies[-1]:
            copy.start()
    key = value = jnp.zeros((rows, width), F32)
    leaving = []
    for j in range(steps):
        for copy in copies[j]:
            copy.wait()
        key += mm(h_s[j], wk_s[j])
        value += mm(h_s[j], wv_s[j])
        turned[j] = h_s[j].T
        for p in range(pairs):
            for which, out in ((core, keep_ref), (1 - core, send_ref)):
                at = pl.ds(pl.multiple_of((2 * p + which) * chunk, chunk), chunk)
                there = out.at[j * pairs + p]
                sem = out_sems.at[j, p, 0 if out is keep_ref else 1]
                leaving.append(pltpu.make_async_copy(turned.at[j, at], there, sem))
                leaving[-1].start()
    for j in range(steps // 2):
        there = mine_ref.at[pl.ds(j * tile, tile)]
        away = (1 - half) * (steps // 2) + j

        @pl.when(core == 0)
        def _():
            pltpu.make_async_copy(wk_s.at[away], there, mine_sems.at[j]).start()

        @pl.when(core != 0)
        def _():
            pltpu.make_async_copy(wv_s.at[away], there, mine_sems.at[j]).start()

        leaving.append(pltpu.make_async_copy(wk_s.at[away], there, mine_sems.at[j]))
    for g, out in enumerate(outs):
        out[0] = key[:, g * HD : (g + 1) * HD].astype(BF)
        out[1] = value[:, g * HD : (g + 1) * HD].astype(BF)
    for copy in leaving:
        copy.wait()


def project(at, hidden, w_key, w_value, parts):
    rows, depth = hidden.shape
    width = w_key.shape[1]
    steps = 4
    tile = depth // steps
    chunk = depth // parts
    groups = width // HD
    far = pl.BlockSpec(memory_space=pltpu.HBM)
    turned = jax.ShapeDtypeStruct((parts // 2, chunk, rows), BF)
    return pl.pallas_call(
        functools.partial(project_kernel, groups),
        out_shape=[jax.ShapeDtypeStruct((2, rows, HD), BF)] * groups
        + [turned, turned, jax.ShapeDtypeStruct((depth // 2, width), BF)],
        in_specs=[pl.BlockSpec(memory_space=pltpu.SMEM)] + [far] * 3,
        out_specs=[RESIDENT] * groups + [far] * 3,
        scratch_shapes=[
            pltpu.VMEM((steps, rows, tile), BF),
            pltpu.VMEM((steps, tile, width), BF),
            pltpu.VMEM((steps, tile, width), BF),
            pltpu.VMEM((steps, tile, rows), BF),
            pltpu.SemaphoreType.DMA((steps, 3)),
            pltpu.SemaphoreType.DMA((steps, tile // (2 * chunk), 2)),
            pltpu.SemaphoreType.DMA((steps // 2,)),
        ],
        compiler_params=pltpu.CompilerParams(vmem_limit_bytes=WHOLE),
        cost_estimate=pl.CostEstimate(
            flops=4 * rows * depth * width,
            bytes_accessed=4 * depth * (rows + width),
            transcendentals=0,
        ),
        name="project",
    )(at, hidden, w_key, w_value)


def attend_kernel(heads, sel_ref, len_ref, q_ref, do_ref, *rest):
    kv_refs, (rk_ref, rv_ref), rest = rest[:REACH], rest[REACH : REACH + 2], rest[REACH + 2 :]
    (o_ref, dq_ref, rdk_ref, rdv_ref, *part_refs) = rest[-13 - REACH : -9]
    (prompt_s, sems, k_s, v_s, kt_s, vt_s, dk_s, dv_s, first_s) = rest[-9:]
    r = pl.program_id(0)
    plen = kv_refs[0].shape[1]
    rlen = q_ref.shape[0]

    @pl.when(r == 0)
    def _():
        for slot in range(prompt_s.shape[0]):
            for j, ref in enumerate(kv_refs):

                @pl.when(sel_ref[slot] == j)
                def _():
                    pltpu.make_async_copy(ref, prompt_s.at[slot], sems.at[slot]).start()

    pltpu.make_async_copy(kv_refs[0], prompt_s.at[r], sems.at[r]).wait()
    k_s[:plen] = prompt_s[r, 0]
    v_s[:plen] = prompt_s[r, 1]
    k_s[plen:] = rk_ref[...]
    v_s[plen:] = rv_ref[...]
    kt_s[...] = k_s[...].T
    vt_s[:HD] = v_s[...].T
    vt_s[HD:] = jnp.ones((ONES, vt_s.shape[1]), BF)
    scale = HD**-0.5
    c = scale * LOG2E
    live = lax.broadcasted_iota(jnp.int32, (1, rlen), 1) < len_ref[r]
    livef = live.astype(F32)
    key_pos = lax.broadcasted_iota(jnp.int32, (rlen, rlen), 0)
    allowed = key_pos <= lax.broadcasted_iota(jnp.int32, (rlen, rlen), 1)
    span = range(heads)
    cols = [pl.ds(h * HD, HD) for h in span]
    scores = [mm(k_s[...], q_ref[:, cols[h]], NT) for h in span]
    grown, rounded = [], []
    for h in span:
        sp = scores[h][:plen]
        sr = jnp.where(allowed, scores[h][plen:], -jnp.inf)
        m = jnp.maximum(jnp.max(sp, axis=0, keepdims=True), jnp.max(sr, axis=0, keepdims=True))
        e = jnp.concatenate([jnp.exp2((sp - m) * c), jnp.exp2((sr - m) * c)], axis=0)
        grown.append(e)
        rounded.append(e.astype(BF))
    outs, douts = [], []
    for h in span:
        both = mm(vt_s[...], rounded[h])
        inv = livef / both[HD : HD + 1]
        ot = both[:HD] * inv
        outs.append(ot)
        o_ref[:, cols[h]] = ot.T.astype(BF)
        douts.append((do_ref[:, cols[h]].T.astype(F32) * inv).astype(BF))
    dss = []
    for h in span:
        delta = jnp.sum(douts[h].astype(F32) * outs[h], axis=0, keepdims=True)
        dss.append((grown[h] * (mm(v_s[...], douts[h]) - delta)).astype(BF))
    for h in span:
        dq_ref[:, cols[h]] = (mm(kt_s[...], dss[h]) * scale).T.astype(BF)
    dv_s[...] = mm(jnp.concatenate(rounded, axis=1), jnp.concatenate(douts, axis=1), NT)
    dk_s[...] = mm(
        jnp.concatenate(dss, axis=1), jnp.concatenate([q_ref[:, cols[h]] for h in span], axis=0)
    )
    rdk_ref[...] = (dk_s[plen:] * scale).astype(BF)
    rdv_ref[...] = dv_s[plen:].astype(BF)

    @pl.when(r == 0)
    def _():
        first_s[0] = dk_s[:plen]
        first_s[1] = dv_s[:plen]

    @pl.when(r == 1)
    def _():
        one, two = sel_ref[0], sel_ref[1]
        for j, part_ref in enumerate(part_refs):

            @pl.when((one != j) & (two != j))
            def _():
                part_ref[...] = jnp.zeros(part_ref.shape, BF)

            @pl.when((one == j) & (two != j))
            def _():
                part_ref[0] = (first_s[0] * scale).astype(BF)
                part_ref[1] = first_s[1].astype(BF)

            @pl.when((one != j) & (two == j))
            def _():
                part_ref[0] = (dk_s[:plen] * scale).astype(BF)
                part_ref[1] = dv_s[:plen].astype(BF)

            @pl.when((one == j) & (two == j))
            def _():
                part_ref[0] = ((first_s[0] + dk_s[:plen]) * scale).astype(BF)
                part_ref[1] = (first_s[1] + dv_s[:plen]).astype(BF)


def attend(g, sel, lengths, q, dout, kvs, rk, rv, prev):
    rows, width = q.shape
    slots = sel.shape[0]
    rlen = rows // slots
    gw = width // (rk.shape[1] // HD)
    heads = gw // HD
    plen = kvs[0].shape[1]
    klen = plen + rlen
    wide = pl.BlockSpec((rlen, gw), lambda r, *_: (r, g))
    narrow = pl.BlockSpec((rlen, HD), lambda r, *_: (r, g))
    ins = [q, dout, *kvs, rk, rv]
    in_specs = [wide, wide] + [pl.BlockSpec(memory_space=pltpu.HBM)] * REACH + [narrow, narrow]
    aliases = {}
    if prev is not None:
        aliases = {2 + len(ins) + i: i for i in range(4)}
        ins += list(prev)
        in_specs += [pl.BlockSpec(memory_space=pl.ANY)] * 4
    return pl.pallas_call(
        functools.partial(attend_kernel, heads),
        out_shape=[jax.ShapeDtypeStruct(q.shape, BF)] * 2
        + [jax.ShapeDtypeStruct(rk.shape, BF)] * 2
        + [jax.ShapeDtypeStruct((2, plen, HD), BF)] * REACH,
        grid_spec=pltpu.PrefetchScalarGridSpec(
            num_scalar_prefetch=2,
            grid=(slots,),
            in_specs=in_specs,
            out_specs=[wide, wide, narrow, narrow]
            + [pl.BlockSpec((2, plen, HD), lambda r, *_: (0, 0, 0))] * REACH,
            scratch_shapes=[
                pltpu.VMEM((slots, 2, plen, HD), BF),
                pltpu.SemaphoreType.DMA((slots,)),
            ]
            + [pltpu.VMEM((klen, HD), BF)] * 2
            + [pltpu.VMEM((HD, klen), BF), pltpu.VMEM((HD + ONES, klen), BF)]
            + [pltpu.VMEM((klen, HD), F32)] * 2
            + [pltpu.VMEM((2, plen, HD), F32)],
        ),
        input_output_aliases=aliases,
        compiler_params=pltpu.CompilerParams(vmem_limit_bytes=WHOLE),
        cost_estimate=pl.CostEstimate(
            flops=slots * heads * 24 * rlen * klen * HD,
            bytes_accessed=8 * MIB,
            transcendentals=slots * heads * rlen * klen,
        ),
        name=f"attend_{g}",
    )(sel, lengths, *ins)


def weight_kernel(index_ref, near_ref, far_ref, own_ref, pair_ref, *rest):
    count = near_ref.shape[0] // 2
    arrived, outs = (rest[0], rest[1:]) if len(rest) > 1 else (None, rest)
    own, pair = own_ref[...], pair_ref[...]
    for i in range(count):
        at = i ^ index_ref[1]
        chunk = 2 * at + index_ref[0]
        total = mm(near_ref[chunk], own) + mm(far_ref[chunk], pair)
        if arrived is not None:
            total += arrived[at].astype(F32)
        if len(outs) == 2:
            outs[i % 2][i // 2] = total.astype(BF)
        else:
            outs[0][at] = total.astype(BF)


def weight_terms(index, near, far, own, pair, arrived):
    count, chunk, rows = near.shape
    count //= 2
    ins = [near, far, own, pair]
    if arrived is not None:
        ins.append(arrived)
    if arrived is not None and count == REACH:
        out_shape = [jax.ShapeDtypeStruct((count // 2, chunk, 2 * HD), BF)] * 2
        out_specs = [RESIDENT] * 2
    else:
        out_shape = jax.ShapeDtypeStruct((count, chunk, 2 * HD), BF)
        out_specs = RESIDENT
    return pl.pallas_call(
        weight_kernel,
        out_shape=out_shape,
        in_specs=[pl.BlockSpec(memory_space=pltpu.SMEM)] + [RESIDENT] * len(ins),
        out_specs=out_specs,
        compiler_params=pltpu.CompilerParams(vmem_limit_bytes=VMEM),
        cost_estimate=pl.CostEstimate(
            flops=8 * rows * count * chunk * HD,
            bytes_accessed=4 * count * chunk * (rows + 2 * HD),
            transcendentals=0,
        ),
        name="weight_keep" if arrived is not None else "weight_send",
    )(index, *ins)


def halve(held, index, bit):
    count = held.shape[0]
    while count > 1:
        mine = (index // bit) % 2
        split = held.reshape(count // 2, 2, *held.shape[1:])
        out = lax.dynamic_index_in_dim(split, 1 - mine, 1, keepdims=False).astype(BF)
        stay = lax.dynamic_index_in_dim(split, mine, 1, keepdims=False).astype(F32)
        held = stay + permute(out, "dp", lambda i: i ^ bit, "terms_halved").astype(F32)
        count //= 2
        bit *= 2
    return held[0]


def place_index(index):
    return (index // 2) % 2, index // 4, jnp.zeros_like(index)


def send_terms(index, near, far, own, pair):
    bit, _, zero = place_index(index)
    return weight_terms(jnp.stack([1 - bit, zero]), near, far, own, pair, None)


def keep_terms(index, near, far, own, pair, arrived):
    bit, place, zero = place_index(index)
    if near.shape[0] // 2 != REACH:
        held = weight_terms(jnp.stack([bit, zero]), near, far, own, pair, arrived)
        return [halve(held, index, 4)]
    kept, sent = weight_terms(jnp.stack([bit, place]), near, far, own, pair, arrived)
    return [kept, permute(sent, "dp", lambda i: i ^ 4, "terms_z1")]


def cross_terms(held):
    if len(held) == 1:
        return held
    kept, sent = held
    two = (kept[1].astype(F32) + sent[1].astype(F32)).astype(BF)
    return [kept[0], sent[0], permute(two, "dp", lambda i: i ^ 8, "terms_z2")]


def hidden_kernel(groups, at_ref, *rest):
    owns, fars, rest = rest[:groups], rest[groups : 2 * groups], rest[2 * groups :]
    (wk_ref, wv_ref, wa_ref, wb_ref, out_ref, grads) = rest
    cols = wa_ref.shape[0]
    step = pl.program_id(0)
    tile = out_ref.shape[1]

    @pl.when(step == 0)
    def _():
        first = at_ref[1]
        for g in range(groups):
            at = pl.ds(g * HD, HD)
            for j in range(2):
                grads[j, :, at] = owns[g][:, j * HD : (j + 1) * HD]
                away = pl.multiple_of(jnp.where(first == 0, j, 1 - j) * HD, HD)
                grads[2 + j, :, at] = fars[g][:, pl.ds(away, HD)]

    near = pl.ds(pl.multiple_of(at_ref[0] * cols + step * tile, tile), tile)
    away = pl.ds(pl.multiple_of(step * tile, tile), tile)
    total = mm(grads[0], wk_ref[near, :], NT) + mm(grads[1], wv_ref[near, :], NT)
    total += mm(grads[2], wa_ref[away, :], NT) + mm(grads[3], wb_ref[away, :], NT)
    out_ref[...] = total.astype(BF)


def hidden_grads(at, owns, fars, w_key, w_value, far_a, far_b):
    groups = len(owns)
    rows = owns[0].shape[0]
    cols, width = far_a.shape
    tile = 512
    return pl.pallas_call(
        functools.partial(hidden_kernel, groups),
        out_shape=jax.ShapeDtypeStruct((rows, cols), BF),
        grid_spec=pltpu.PrefetchScalarGridSpec(
            num_scalar_prefetch=1,
            grid=(cols // tile,),
            in_specs=[RESIDENT] * (2 * groups + 4),
            out_specs=pl.BlockSpec((rows, tile), lambda i, at: (0, i)),
            scratch_shapes=[pltpu.VMEM((4, rows, width), BF)],
        ),
        compiler_params=pltpu.CompilerParams(vmem_limit_bytes=VMEM),
        cost_estimate=pl.CostEstimate(
            flops=8 * rows * cols * width,
            bytes_accessed=2 * cols * (rows + 4 * width),
            transcendentals=0,
        ),
        name="hidden_grads",
    )(at, *owns, *fars, w_key, w_value, far_a, far_b)


def total_grad(own, shares):
    total = own.astype(F32)
    for share in shares:
        total += share.astype(F32)
    return jnp.concatenate([total[0], total[1]], axis=-1).astype(BF)


def body(
    prompt_hidden,
    w_key,
    w_value,
    queries,
    resp_key,
    resp_value,
    cotangent,
    group_offset,
    resp_length,
):
    size = lax.axis_size("dp")
    index = lax.axis_index("dp")
    core = index % 2
    half = lax.axis_index("mp")
    groups = w_key.shape[1] // HD
    cols = w_key.shape[0] // 2

    def other(i):
        return (i + 1) % size if i % 2 == 0 else (i + 3) % size

    def back(i):
        return (i - 1) % size if i % 2 == 1 else (i - 3) % size

    def cross(i):
        return (i - 1) % size if i % 2 == 0 else (i - 3) % size

    sel = jnp.where((group_offset % 2 == 1) & (core == 0), 4 - group_offset, group_offset)

    at = jnp.stack([half, core])
    *pairs, near, turned, mine = project(at, prompt_hidden, w_key, w_value, size)
    two = permute(pairs[0], "dp", lambda i: (i + 2) % size, "pair_two")
    one = permute(pairs[0], "dp", other, "pair_other")
    received = [[pairs[0], one, two, permute(two, "dp", lambda i: i ^ 1, "pair_core")]]
    far_a = permute(mine, "mp", lambda i: 1 - i, "weights_y")
    far = permute(turned, "dp", lambda i: i ^ 1, "turned_core")
    later = after(pairs[1], two)
    received.append(
        [
            later,
            permute(later, "dp", other, "pair_other"),
            permute(later, "dp", lambda i: (i + 2) % size, "pair_two"),
            permute(later, "dp", lambda i: (i + (1 if i % 2 else 3)) % size, "pair_cross"),
        ]
    )

    *prev, mine_0, other_0, two_0, core_0 = attend(
        0, sel, resp_length, queries, cotangent, received[0], resp_key, resp_value, None
    )
    shares = [
        permute(other_0, "dp", back, "grad_other"),
        permute(two_0, "dp", lambda i: (i - 2) % size, "grad_two"),
        permute(core_0, "dp", cross, "grad_cross"),
    ]
    received[1], far, far_a, prev = after((received[1], far, far_a, prev), mine_0)
    *prev, mine_1, other_1, two_1, core_1 = attend(
        1, sel, resp_length, queries, cotangent, received[1], resp_key, resp_value, prev
    )
    far_b = permute(far_a, "dp", lambda i: i ^ 1, "weights_core")
    swapped = permute(core_1, "dp", lambda i: i ^ 1, "grad_core")
    shares_1 = [permute(other_1, "dp", back, "grad_other")]

    def along_x(i):
        return i ^ 2

    own = [total_grad(after(mine_0, mine_1), shares)]
    pair = [permute(own[0], "dp", lambda i: i ^ 1, "own_core")]
    two = after((two_1.astype(F32) + swapped.astype(F32)).astype(BF), own[0])
    shares_1.append(permute(two, "dp", lambda i: (i - 2) % size, "grad_two"))
    sent = [send_terms(index, near, far, after(own[0], two), pair[0])]
    arrived = [permute(sent[0], "dp", along_x, "terms_x")]

    own.append(total_grad(after(mine_1, sent[0]), shares_1))
    pair.append(permute(own[1], "dp", lambda i: i ^ 1, "own_core"))
    sent.append(send_terms(index, near, far, own[1], pair[1]))
    arrived.append(permute(sent[1], "dp", along_x, "terms_x"))
    away = [permute(grad, "mp", lambda i: 1 - i, "own_y") for grad in own]

    held = [keep_terms(index, near, far, own[0], pair[0], after(arrived[0], sent[1]))]
    hidden_grad = hidden_grads(
        at, after(own, held[0][0]), away, w_key, w_value, far_a, far_b
    )
    terms = [cross_terms(after(held[0], hidden_grad))]
    held.append(keep_terms(index, near, far, own[1], pair[1], after(arrived[1], terms[0][:2][-1])))
    terms.append(cross_terms(held[1]))
    weight_grads = [sum(t.astype(F32) for t in term) for term in terms]
    return (
        *prev,
        hidden_grad,
        jnp.concatenate([t[:, :HD] for t in weight_grads], axis=-1),
        jnp.concatenate([t[:, HD:] for t in weight_grads], axis=-1),
    )


def solution(mesh):
    placed = (
        P("dp", None),
        P(None, "mp"),
        P(None, "mp"),
        P("dp", "mp"),
        P("dp", "mp"),
        P("dp", "mp"),
        P("dp", "mp"),
        P("dp"),
        P("dp"),
    )
    return jax.shard_map(
        body,
        mesh=mesh,
        in_specs=placed,
        out_specs=(P("dp", "mp"),) * 7,
        check_vma=False,
    )
```

```python
import functools
import math

import jax
import jax.numpy as jnp
from jax import lax
from jax.experimental import pallas as pl
from jax.experimental.pallas import tpu as pltpu
from jax.sharding import PartitionSpec as P

HD = 128
REACH = 4
ONES = 16
LOG2E = 1.4426950408889634
BF = jnp.bfloat16
F32 = jnp.float32
NT = (((1,), (1,)), ((), ()))
NN = (((1,), (0,)), ((), ()))
TN = (((0,), (0,)), ((), ()))
MIB = 1024 * 1024
VMEM = 16 * MIB
SMALL = 12 * MIB
WHOLE = 58 * MIB
ATTEND = 36 * MIB
RESIDENT = pl.BlockSpec(memory_space=pltpu.VMEM)


def mm(a, b, dims=NN):
    return lax.dot_general(a, b, dims, preferred_element_type=F32)


def permute(block, axis, target, name):
    with jax.named_scope(name):
        return lax.ppermute(block, axis, [(i, target(i)) for i in range(lax.axis_size(axis))])


def after(values, *others):
    return lax.optimization_barrier((values, others))[0]


def project_kernel(groups, at_ref, h_ref, wk_ref, wv_ref, *rest):
    outs, (keep_ref, send_ref, mine_ref), rest = rest[:groups], rest[groups : groups + 3], rest[groups + 3 :]
    h_s, wk_s, wv_s, turned, in_sems, out_sems, mine_sems = rest
    steps, rows, tile = h_s.shape
    width = wk_s.shape[2]
    chunk = keep_ref.shape[1]
    pairs = tile // (2 * chunk)
    half, core = at_ref[0], at_ref[1]
    copies = []
    for j in range(steps):
        at = pl.ds(j * tile, tile)
        copies.append(
            [
                pltpu.make_async_copy(h_ref.at[:, at], h_s.at[j], in_sems.at[j, 0]),
                pltpu.make_async_copy(wk_ref.at[at], wk_s.at[j], in_sems.at[j, 1]),
                pltpu.make_async_copy(wv_ref.at[at], wv_s.at[j], in_sems.at[j, 2]),
            ]
        )
        for copy in copies[-1]:
            copy.start()
    key = value = jnp.zeros((rows, width), F32)
    leaving = []
    for j in range(steps):
        for copy in copies[j]:
            copy.wait()
        key += mm(h_s[j], wk_s[j])
        value += mm(h_s[j], wv_s[j])
        turned[j] = h_s[j].T
        for p in range(pairs):
            for which, out in ((core, keep_ref), (1 - core, send_ref)):
                at = pl.ds(pl.multiple_of((2 * p + which) * chunk, chunk), chunk)
                there = out.at[j * pairs + p]
                sem = out_sems.at[j, p, 0 if out is keep_ref else 1]
                leaving.append(pltpu.make_async_copy(turned.at[j, at], there, sem))
                leaving[-1].start()
    for j in range(steps // 2):
        there = mine_ref.at[pl.ds(j * tile, tile)]
        away = (1 - half) * (steps // 2) + j

        @pl.when(core == 0)
        def _():
            pltpu.make_async_copy(wk_s.at[away], there, mine_sems.at[j]).start()

        @pl.when(core != 0)
        def _():
            pltpu.make_async_copy(wv_s.at[away], there, mine_sems.at[j]).start()

        leaving.append(pltpu.make_async_copy(wk_s.at[away], there, mine_sems.at[j]))
    for g, out in enumerate(outs):
        out[0] = key[:, g * HD : (g + 1) * HD].astype(BF)
        out[1] = value[:, g * HD : (g + 1) * HD].astype(BF)
    for copy in leaving:
        copy.wait()


def project(at, hidden, w_key, w_value, parts):
    rows, depth = hidden.shape
    width = w_key.shape[1]
    steps = 4
    tile = depth // steps
    chunk = depth // parts
    groups = width // HD
    far = pl.BlockSpec(memory_space=pltpu.HBM)
    turned = jax.ShapeDtypeStruct((parts // 2, chunk, rows), BF)
    return pl.pallas_call(
        functools.partial(project_kernel, groups),
        out_shape=[jax.ShapeDtypeStruct((2, rows, HD), BF)] * groups
        + [turned, turned, jax.ShapeDtypeStruct((depth // 2, width), BF)],
        in_specs=[pl.BlockSpec(memory_space=pltpu.SMEM)] + [far] * 3,
        out_specs=[RESIDENT] * groups + [far] * 3,
        scratch_shapes=[
            pltpu.VMEM((steps, rows, tile), BF),
            pltpu.VMEM((steps, tile, width), BF),
            pltpu.VMEM((steps, tile, width), BF),
            pltpu.VMEM((steps, tile, rows), BF),
            pltpu.SemaphoreType.DMA((steps, 3)),
            pltpu.SemaphoreType.DMA((steps, tile // (2 * chunk), 2)),
            pltpu.SemaphoreType.DMA((steps // 2,)),
        ],
        compiler_params=pltpu.CompilerParams(vmem_limit_bytes=WHOLE),
        cost_estimate=pl.CostEstimate(
            flops=4 * rows * depth * width,
            bytes_accessed=4 * depth * (rows + width),
            transcendentals=0,
        ),
        name="project",
    )(at, hidden, w_key, w_value)


def attend_kernel(heads, loads, sel_ref, len_ref, q_ref, do_ref, *rest):
    if loads:
        sources, landed = rest[REACH + 2 : REACH + 2 + loads], rest[-10 - loads : -10]
        load_sems = rest[-1]
        rest = rest[: REACH + 2] + rest[REACH + 2 + loads : -10 - loads] + rest[-10:-1]
        moves = [
            pltpu.make_async_copy(src, dst, load_sems.at[i])
            for i, (src, dst) in enumerate(zip(sources, landed))
        ]

        @pl.when(pl.program_id(0) == 0)
        def _():
            for move in moves:
                move.start()

        @pl.when(pl.program_id(0) == pl.num_programs(0) - 1)
        def _():
            for move in moves:
                move.wait()

    kv_refs, (rk_ref, rv_ref), rest = rest[:REACH], rest[REACH : REACH + 2], rest[REACH + 2 :]
    (o_ref, dq_ref, rdk_ref, rdv_ref, *part_refs) = rest[-13 - REACH : -9]
    (prompt_s, sems, k_s, v_s, kt_s, vt_s, dk_s, dv_s, first_s) = rest[-9:]
    r = pl.program_id(0)
    plen = kv_refs[0].shape[1]
    rlen = q_ref.shape[0]

    @pl.when(r == 0)
    def _():
        for slot in range(prompt_s.shape[0]):
            for j, ref in enumerate(kv_refs):

                @pl.when(sel_ref[slot] == j)
                def _():
                    pltpu.make_async_copy(ref, prompt_s.at[slot], sems.at[slot]).start()

    pltpu.make_async_copy(kv_refs[0], prompt_s.at[r], sems.at[r]).wait()
    k_s[:plen] = prompt_s[r, 0]
    v_s[:plen] = prompt_s[r, 1]
    k_s[plen:] = rk_ref[...]
    v_s[plen:] = rv_ref[...]
    kt_s[...] = k_s[...].T
    vt_s[:HD] = v_s[...].T
    vt_s[HD:] = jnp.ones((ONES, vt_s.shape[1]), BF)
    scale = HD**-0.5
    c = scale * LOG2E
    live = lax.broadcasted_iota(jnp.int32, (1, rlen), 1) < len_ref[r]
    livef = live.astype(F32)
    key_pos = lax.broadcasted_iota(jnp.int32, (rlen, rlen), 0)
    allowed = key_pos <= lax.broadcasted_iota(jnp.int32, (rlen, rlen), 1)
    span = range(heads)
    cols = [pl.ds(h * HD, HD) for h in span]
    scores = [mm(k_s[...], q_ref[:, cols[h]], NT) for h in span]
    grown, rounded = [], []
    for h in span:
        sp = scores[h][:plen]
        sr = jnp.where(allowed, scores[h][plen:], -jnp.inf)
        m = jnp.maximum(jnp.max(sp, axis=0, keepdims=True), jnp.max(sr, axis=0, keepdims=True))
        e = jnp.concatenate([jnp.exp2((sp - m) * c), jnp.exp2((sr - m) * c)], axis=0)
        grown.append(e)
        rounded.append(e.astype(BF))
    outs, douts = [], []
    for h in span:
        both = mm(vt_s[...], rounded[h])
        inv = livef / both[HD : HD + 1]
        ot = both[:HD] * inv
        outs.append(ot)
        o_ref[:, cols[h]] = ot.T.astype(BF)
        douts.append((do_ref[:, cols[h]].T.astype(F32) * inv).astype(BF))
    dss = []
    for h in span:
        delta = jnp.sum(douts[h].astype(F32) * outs[h], axis=0, keepdims=True)
        dss.append((grown[h] * (mm(v_s[...], douts[h]) - delta)).astype(BF))
    for h in span:
        dq_ref[:, cols[h]] = (mm(kt_s[...], dss[h]) * scale).T.astype(BF)
    dv_s[...] = mm(jnp.concatenate(rounded, axis=1), jnp.concatenate(douts, axis=1), NT)
    dk_s[...] = mm(
        jnp.concatenate(dss, axis=1), jnp.concatenate([q_ref[:, cols[h]] for h in span], axis=0)
    )
    rdk_ref[...] = (dk_s[plen:] * scale).astype(BF)
    rdv_ref[...] = dv_s[plen:].astype(BF)

    @pl.when(r == 0)
    def _():
        first_s[0] = dk_s[:plen]
        first_s[1] = dv_s[:plen]

    @pl.when(r == 1)
    def _():
        one, two = sel_ref[0], sel_ref[1]
        for j, part_ref in enumerate(part_refs):

            @pl.when((one != j) & (two != j))
            def _():
                part_ref[...] = jnp.zeros(part_ref.shape, BF)

            @pl.when((one == j) & (two != j))
            def _():
                part_ref[0] = (first_s[0] * scale).astype(BF)
                part_ref[1] = first_s[1].astype(BF)

            @pl.when((one != j) & (two == j))
            def _():
                part_ref[0] = (dk_s[:plen] * scale).astype(BF)
                part_ref[1] = dv_s[:plen].astype(BF)

            @pl.when((one == j) & (two == j))
            def _():
                part_ref[0] = ((first_s[0] + dk_s[:plen]) * scale).astype(BF)
                part_ref[1] = (first_s[1] + dv_s[:plen]).astype(BF)


def attend(g, sel, lengths, q, dout, kvs, rk, rv, prev, loads=()):
    rows, width = q.shape
    slots = sel.shape[0]
    rlen = rows // slots
    gw = width // (rk.shape[1] // HD)
    heads = gw // HD
    plen = kvs[0].shape[1]
    klen = plen + rlen
    wide = pl.BlockSpec((rlen, gw), lambda r, *_: (r, g))
    narrow = pl.BlockSpec((rlen, HD), lambda r, *_: (r, g))
    ins = [q, dout, *kvs, rk, rv]
    in_specs = [wide, wide] + [pl.BlockSpec(memory_space=pltpu.HBM)] * REACH + [narrow, narrow]
    ins += list(loads)
    in_specs += [pl.BlockSpec(memory_space=pltpu.HBM)] * len(loads)
    aliases = {}
    if prev is not None:
        aliases = {2 + len(ins) + i: i for i in range(4)}
        ins += list(prev)
        in_specs += [pl.BlockSpec(memory_space=pl.ANY)] * 4
    return pl.pallas_call(
        functools.partial(attend_kernel, heads, len(loads)),
        out_shape=[jax.ShapeDtypeStruct(q.shape, BF)] * 2
        + [jax.ShapeDtypeStruct(rk.shape, BF)] * 2
        + [jax.ShapeDtypeStruct((2, plen, HD), BF)] * REACH
        + [jax.ShapeDtypeStruct(x.shape, x.dtype) for x in loads],
        grid_spec=pltpu.PrefetchScalarGridSpec(
            num_scalar_prefetch=2,
            grid=(slots,),
            in_specs=in_specs,
            out_specs=[wide, wide, narrow, narrow]
            + [pl.BlockSpec((2, plen, HD), lambda r, *_: (0, 0, 0))] * REACH
            + [RESIDENT] * len(loads),
            scratch_shapes=[
                pltpu.VMEM((slots, 2, plen, HD), BF),
                pltpu.SemaphoreType.DMA((slots,)),
            ]
            + [pltpu.VMEM((klen, HD), BF)] * 2
            + [pltpu.VMEM((HD, klen), BF), pltpu.VMEM((HD + ONES, klen), BF)]
            + [pltpu.VMEM((klen, HD), F32)] * 2
            + [pltpu.VMEM((2, plen, HD), F32)]
            + [pltpu.SemaphoreType.DMA((len(loads),))] * bool(loads),
        ),
        input_output_aliases=aliases,
        compiler_params=pltpu.CompilerParams(vmem_limit_bytes=ATTEND),
        cost_estimate=pl.CostEstimate(
            flops=slots * heads * 24 * rlen * klen * HD,
            bytes_accessed=8 * MIB,
            transcendentals=slots * heads * rlen * klen,
        ),
        name=f"attend_{g}",
    )(sel, lengths, *ins)


def weight_kernel(first, at_ref, near_ref, far_ref, own_ref, pair_ref, *rest):
    count = at_ref.shape[0]
    arrived, outs = (rest[0], rest[1:]) if rest[0].shape[0] == count and len(rest) > 1 else (None, rest)
    width = outs[0].shape[2]
    own = own_ref[:, first : first + width]
    pair = pair_ref[:, first : first + width]
    each = outs[0].shape[0]
    for i in range(count):
        chunk = at_ref[i]
        total = mm(near_ref[chunk], own) + mm(far_ref[chunk], pair)
        if arrived is not None:
            total += arrived[i].astype(F32)
        outs[i // each][i % each] = total.astype(BF)


def weight_terms(at, near, far, grads, columns, arrived=None, parts=1):
    own, pair = grads
    chunk, rows = near.shape[1:]
    count = at.shape[0]
    first, width = columns
    ins = [near, far, own, pair] + ([] if arrived is None else [arrived])
    return pl.pallas_call(
        functools.partial(weight_kernel, first),
        out_shape=[jax.ShapeDtypeStruct((count // parts, chunk, width), BF)] * parts,
        in_specs=[pl.BlockSpec(memory_space=pltpu.SMEM)] + [RESIDENT] * len(ins),
        out_specs=[RESIDENT] * parts,
        compiler_params=pltpu.CompilerParams(vmem_limit_bytes=SMALL),
        cost_estimate=pl.CostEstimate(
            flops=4 * rows * count * chunk * width,
            bytes_accessed=4 * count * chunk * (rows + width),
            transcendentals=0,
        ),
        name="weight_terms",
    )(at, *ins)


def add(one, two):
    return one.astype(F32) + two.astype(F32)


def hidden_kernel(groups, at_ref, *rest):
    owns, fars, rest = rest[:groups], rest[groups : 2 * groups], rest[2 * groups :]
    (wk_ref, wv_ref, wa_ref, wb_ref, out_ref, grads, weights, done, in_sems, out_sems) = rest
    cols = wa_ref.shape[0]
    steps, tile = weights.shape[1:3]
    copies = []
    for step in range(steps):
        near = pl.ds(pl.multiple_of(at_ref[0] * cols + step * tile, tile), tile)
        away = pl.ds(step * tile, tile)
        sources = (wk_ref.at[near], wv_ref.at[near], wa_ref.at[away], wb_ref.at[away])
        copies.append(
            [
                pltpu.make_async_copy(source, weights.at[j, step], in_sems.at[j, step])
                for j, source in enumerate(sources)
            ]
        )
        for copy in copies[-1]:
            copy.start()
    first = at_ref[1]
    for g in range(groups):
        at = pl.ds(g * HD, HD)
        for j in range(2):
            grads[j, :, at] = owns[g][:, j * HD : (j + 1) * HD]
            away = pl.multiple_of(jnp.where(first == 0, j, 1 - j) * HD, HD)
            grads[2 + j, :, at] = fars[g][:, pl.ds(away, HD)]
    leaving = []
    for step in range(steps):
        for copy in copies[step]:
            copy.wait()
        total = mm(grads[0], weights[0, step], NT)
        for j in range(1, 4):
            total += mm(grads[j], weights[j, step], NT)
        done[step] = total.astype(BF)
        there = out_ref.at[:, pl.ds(step * tile, tile)]
        leaving.append(pltpu.make_async_copy(done.at[step], there, out_sems.at[step]))
        leaving[-1].start()
    for copy in leaving:
        copy.wait()


def hidden_grads(at, owns, fars, w_key, w_value, far_a, far_b):
    groups = len(owns)
    rows = owns[0].shape[0]
    cols, width = far_a.shape
    tile = 512
    steps = cols // tile
    far = pl.BlockSpec(memory_space=pltpu.HBM)
    return pl.pallas_call(
        functools.partial(hidden_kernel, groups),
        out_shape=jax.ShapeDtypeStruct((rows, cols), BF),
        in_specs=[pl.BlockSpec(memory_space=pltpu.SMEM)]
        + [RESIDENT] * (2 * groups)
        + [far] * 4,
        out_specs=far,
        scratch_shapes=[
            pltpu.VMEM((4, rows, width), BF),
            pltpu.VMEM((4, steps, tile, width), BF),
            pltpu.VMEM((steps, rows, tile), BF),
            pltpu.SemaphoreType.DMA((4, steps)),
            pltpu.SemaphoreType.DMA((steps,)),
        ],
        compiler_params=pltpu.CompilerParams(vmem_limit_bytes=VMEM),
        cost_estimate=pl.CostEstimate(
            flops=8 * rows * cols * width,
            bytes_accessed=2 * cols * (rows + 4 * width),
            transcendentals=0,
        ),
        name="hidden_grads",
    )(at, *owns, *fars, w_key, w_value, far_a, far_b)


def total_grad(own, shares):
    total = own.astype(F32)
    for share in shares:
        total += share.astype(F32)
    return jnp.concatenate([total[0], total[1]], axis=-1).astype(BF)


def body(
    prompt_hidden,
    w_key,
    w_value,
    queries,
    resp_key,
    resp_value,
    cotangent,
    group_offset,
    resp_length,
):
    size = lax.axis_size("dp")
    index = lax.axis_index("dp")
    core = index % 2
    half = lax.axis_index("mp")
    groups = w_key.shape[1] // HD
    cols = w_key.shape[0] // 2

    def other(i):
        return (i + 1) % size if i % 2 == 0 else (i + 3) % size

    def back(i):
        return (i - 1) % size if i % 2 == 1 else (i - 3) % size

    def cross(i):
        return (i - 1) % size if i % 2 == 0 else (i - 3) % size

    sel = jnp.where((group_offset % 2 == 1) & (core == 0), 4 - group_offset, group_offset)

    at = jnp.stack([half, core])
    *pairs, near, turned, mine = project(at, prompt_hidden, w_key, w_value, size)
    two = permute(pairs[0], "dp", lambda i: (i + 2) % size, "pair_two")
    one = permute(pairs[0], "dp", other, "pair_other")
    received = [[pairs[0], one, two, permute(two, "dp", lambda i: i ^ 1, "pair_core")]]
    far_a = permute(mine, "mp", lambda i: 1 - i, "weights_y")
    far = permute(turned, "dp", lambda i: i ^ 1, "turned_core")
    later = after(pairs[1], two)
    received.append(
        [
            later,
            permute(later, "dp", other, "pair_other"),
            permute(later, "dp", lambda i: (i + 2) % size, "pair_two"),
            permute(later, "dp", lambda i: (i + (1 if i % 2 else 3)) % size, "pair_cross"),
        ]
    )

    *prev, mine_0, other_0, two_0, core_0 = attend(
        0, sel, resp_length, queries, cotangent, received[0], resp_key, resp_value, None
    )
    shares = [
        permute(other_0, "dp", back, "grad_other"),
        permute(two_0, "dp", lambda i: (i - 2) % size, "grad_two"),
        permute(core_0, "dp", cross, "grad_cross"),
    ]
    received[1], far, far_a, prev = after((received[1], far, far_a, prev), mine_0)
    *prev, mine_1, other_1, two_1, core_1, near, far = attend(
        1,
        sel,
        resp_length,
        queries,
        cotangent,
        received[1],
        resp_key,
        resp_value,
        prev,
        (near, far),
    )
    far_b = permute(far_a, "dp", lambda i: i ^ 1, "weights_core")
    swapped = permute(core_1, "dp", lambda i: i ^ 1, "grad_core")
    shares_1 = [permute(other_1, "dp", back, "grad_other")]

    own = [total_grad(after(mine_0, mine_1), shares)]
    pair = [permute(own[0], "dp", lambda i: i ^ 1, "own_core")]
    two = after((two_1.astype(F32) + swapped.astype(F32)).astype(BF), own[0])
    shares_1.append(permute(two, "dp", lambda i: (i - 2) % size, "grad_two"))

    bit, place = (index // 2) % 2, index // 4
    count = near.shape[0]

    def places(shifts, flips):
        return jnp.stack([2 * (place ^ i) + (bit ^ x) for i in shifts for x in flips])

    def along(block, bits, name):
        return permute(block, "dp", lambda i: i ^ bits, name)

    def far_sum(kept, rest, bits):
        while rest:
            sent = jnp.stack([rest[0]] + rest[1:][1::2])
            got = along(sent.astype(BF), bits, "terms_z")
            kept = add(kept, got[0])
            rest = [add(r, g) for r, g in zip(rest[1:][0::2], got[1:])]
            bits *= 2
        return kept

    whole = (0, 2 * HD)
    every = range(count // 2)
    if count // 2 != REACH:
        owns = own + [total_grad(mine_1, shares_1)]
        weight_grads = []
        for grad in owns:
            grads = (grad, permute(grad, "dp", lambda i: i ^ 1, "own_core"))
            (sent,) = weight_terms(places(every, [1]), near, far, grads, whole)
            got = along(sent, 2, "terms_x")
            (held,) = weight_terms(places(every, [0]), near, far, grads, whole, got)
            weight_grads.append(far_sum(held[0], list(held[1:]), 4))
        away = [permute(grad, "mp", lambda i: 1 - i, "own_y") for grad in owns]
        hidden_grad = hidden_grads(at, owns, away, w_key, w_value, far_a, far_b)
        keys = [t[:, :HD] for t in weight_grads]
        values = [t[:, HD:] for t in weight_grads]
        return (
            *prev,
            hidden_grad,
            jnp.concatenate(keys, axis=-1),
            jnp.concatenate(values, axis=-1),
        )

    key, value = (0, HD), (HD, HD)
    near_first, near_then = [0, 2], [1, 3]
    every = near_first + near_then
    grads_0 = (after(own[0], two), pair[0])
    (sent_0,) = weight_terms(places(every, [1]), near, far, grads_0, whole)
    got_0 = along(sent_0, 2, "terms_x")
    away = [permute(after(own[0], sent_0), "mp", lambda i: 1 - i, "own_y")]
    own.append(total_grad(after(mine_1, sent_0, away[0]), shares_1))
    pair.append(permute(own[1], "dp", lambda i: i ^ 1, "own_core"))
    grads_1 = (own[1], pair[1])
    (sent_v,) = weight_terms(places([1, 3], [0, 1]), near, far, grads_1, value)
    got_v = along(sent_v, 4, "terms_z1")
    (sent_k,) = weight_terms(places(every, [1]), near, far, (after(own[1], sent_v), pair[1]), key)
    got_k = along(sent_k, 2, "terms_x")

    held_0, sent_0 = weight_terms(
        places(every, [0]), near, far, grads_0, whole,
        after(got_0, sent_k), 2,
    )
    got_0 = along(sent_0, 4, "terms_z1")
    away.append(permute(after(own[1], held_0), "mp", lambda i: 1 - i, "own_y"))
    held_v, sent_v = weight_terms(
        places(near_first, [0, 1]), near, far, grads_1, value, after(got_v, held_0), 2
    )
    got_v = along(sent_v, 8, "terms_z2")
    held_k, sent_k = weight_terms(
        places(every, [0]), near, far, grads_1, key, after(got_k, held_v, away[1]), 2
    )
    got_k = along(sent_k, 4, "terms_z1")
    two_0 = add(held_0[1], after(got_0, held_k)[1]).astype(BF)
    last_0 = along(two_0, 8, "terms_z2")
    two_v = add(held_v[1], after(got_v, two_0)[1]).astype(BF)
    last_v = along(two_v, 2, "terms_x")
    two_k = add(held_k[1], after(got_k, two_v)[1]).astype(BF)
    last_k = along(two_k, 8, "terms_z2")
    hidden_grad = hidden_grads(
        at, after(own, two_0, two_v, two_k), away, w_key, w_value, far_a, far_b
    )
    last_0, last_v, last_k = after((last_0, last_v, last_k), hidden_grad)
    total_0 = add(add(held_0[0], got_0[0]), last_0)
    total_v = add(add(held_v[0], got_v[0]), last_v)
    total_k = add(add(held_k[0], got_k[0]), last_k)
    return (
        *prev,
        hidden_grad,
        jnp.concatenate([total_0[:, :HD], total_k], axis=-1),
        jnp.concatenate([total_0[:, HD:], total_v], axis=-1),
    )


def solution(mesh):
    placed = (
        P("dp", None),
        P(None, "mp"),
        P(None, "mp"),
        P("dp", "mp"),
        P("dp", "mp"),
        P("dp", "mp"),
        P("dp", "mp"),
        P("dp"),
        P("dp"),
    )
    return jax.shard_map(
        body,
        mesh=mesh,
        in_specs=placed,
        out_specs=(P("dp", "mp"),) * 7,
        check_vma=False,
    )
```

```python
import functools
import math

import jax
import jax.numpy as jnp
from jax import lax
from jax.experimental import pallas as pl
from jax.experimental.pallas import tpu as pltpu
from jax.sharding import PartitionSpec as P

HD = 128
REACH = 4
ONES = 16
LOG2E = 1.4426950408889634
BF = jnp.bfloat16
F32 = jnp.float32
NT = (((1,), (1,)), ((), ()))
NN = (((1,), (0,)), ((), ()))
TN = (((0,), (0,)), ((), ()))
MIB = 1024 * 1024
VMEM = 16 * MIB
SMALL = 12 * MIB
WHOLE = 58 * MIB
ATTEND = 36 * MIB
RESIDENT = pl.BlockSpec(memory_space=pltpu.VMEM)


def mm(a, b, dims=NN):
    return lax.dot_general(a, b, dims, preferred_element_type=F32)


def permute(block, axis, target, name):
    with jax.named_scope(name):
        return lax.ppermute(block, axis, [(i, target(i)) for i in range(lax.axis_size(axis))])


def after(values, *others):
    return lax.optimization_barrier((values, others))[0]


def project_kernel(groups, at_ref, h_ref, wk_ref, wv_ref, *rest):
    outs, (keep_ref, send_ref, mine_ref), rest = rest[:groups], rest[groups : groups + 3], rest[groups + 3 :]
    h_s, wk_s, wv_s, turned, in_sems, out_sems, mine_sems = rest
    steps, rows, tile = h_s.shape
    width = wk_s.shape[2]
    chunk = keep_ref.shape[1]
    pairs = tile // (2 * chunk)
    half, core = at_ref[0], at_ref[1]
    copies = []
    for j in range(steps):
        at = pl.ds(j * tile, tile)
        copies.append(
            [
                pltpu.make_async_copy(h_ref.at[:, at], h_s.at[j], in_sems.at[j, 0]),
                pltpu.make_async_copy(wk_ref.at[at], wk_s.at[j], in_sems.at[j, 1]),
                pltpu.make_async_copy(wv_ref.at[at], wv_s.at[j], in_sems.at[j, 2]),
            ]
        )
        for copy in copies[-1]:
            copy.start()
    key = value = jnp.zeros((rows, width), F32)
    leaving = []
    for j in range(steps):
        for copy in copies[j]:
            copy.wait()
        key += mm(h_s[j], wk_s[j])
        value += mm(h_s[j], wv_s[j])
        turned[j] = h_s[j].T
        for p in range(pairs):
            for which, out in ((core, keep_ref), (1 - core, send_ref)):
                at = pl.ds(pl.multiple_of((2 * p + which) * chunk, chunk), chunk)
                there = out.at[j * pairs + p]
                sem = out_sems.at[j, p, 0 if out is keep_ref else 1]
                leaving.append(pltpu.make_async_copy(turned.at[j, at], there, sem))
                leaving[-1].start()
    for j in range(steps // 2):
        there = mine_ref.at[pl.ds(j * tile, tile)]
        away = (1 - half) * (steps // 2) + j

        @pl.when(core == 0)
        def _():
            pltpu.make_async_copy(wk_s.at[away], there, mine_sems.at[j]).start()

        @pl.when(core != 0)
        def _():
            pltpu.make_async_copy(wv_s.at[away], there, mine_sems.at[j]).start()

        leaving.append(pltpu.make_async_copy(wk_s.at[away], there, mine_sems.at[j]))
    for g, out in enumerate(outs):
        out[0] = key[:, g * HD : (g + 1) * HD].astype(BF)
        out[1] = value[:, g * HD : (g + 1) * HD].astype(BF)
    for copy in leaving:
        copy.wait()


def project(at, hidden, w_key, w_value, parts):
    rows, depth = hidden.shape
    width = w_key.shape[1]
    steps = 4
    tile = depth // steps
    chunk = depth // parts
    groups = width // HD
    far = pl.BlockSpec(memory_space=pltpu.HBM)
    turned = jax.ShapeDtypeStruct((parts // 2, chunk, rows), BF)
    return pl.pallas_call(
        functools.partial(project_kernel, groups),
        out_shape=[jax.ShapeDtypeStruct((2, rows, HD), BF)] * groups
        + [turned, turned, jax.ShapeDtypeStruct((depth // 2, width), BF)],
        in_specs=[pl.BlockSpec(memory_space=pltpu.SMEM)] + [far] * 3,
        out_specs=[RESIDENT] * groups + [far] * 3,
        scratch_shapes=[
            pltpu.VMEM((steps, rows, tile), BF),
            pltpu.VMEM((steps, tile, width), BF),
            pltpu.VMEM((steps, tile, width), BF),
            pltpu.VMEM((steps, tile, rows), BF),
            pltpu.SemaphoreType.DMA((steps, 3)),
            pltpu.SemaphoreType.DMA((steps, tile // (2 * chunk), 2)),
            pltpu.SemaphoreType.DMA((steps // 2,)),
        ],
        compiler_params=pltpu.CompilerParams(vmem_limit_bytes=WHOLE),
        cost_estimate=pl.CostEstimate(
            flops=4 * rows * depth * width,
            bytes_accessed=4 * depth * (rows + width),
            transcendentals=0,
        ),
        name="project",
    )(at, hidden, w_key, w_value)


def attend_kernel(heads, loads, sel_ref, len_ref, q_ref, do_ref, *rest):
    if loads:
        sources, landed = rest[REACH + 2 : REACH + 2 + loads], rest[-11]
        load_sems = rest[-1]
        rest = rest[: REACH + 2] + rest[REACH + 2 + loads : -11] + rest[-10:-1]
        moves = [
            pltpu.make_async_copy(src, landed.at[i], load_sems.at[i])
            for i, src in enumerate(sources)
        ]

        @pl.when(pl.program_id(0) == 0)
        def _():
            for move in moves:
                move.start()

        @pl.when(pl.program_id(0) == pl.num_programs(0) - 1)
        def _():
            for move in moves:
                move.wait()

    kv_refs, (rk_ref, rv_ref), rest = rest[:REACH], rest[REACH : REACH + 2], rest[REACH + 2 :]
    (o_ref, dq_ref, rdk_ref, rdv_ref, *part_refs) = rest[-13 - REACH : -9]
    (prompt_s, sems, k_s, v_s, kt_s, vt_s, dk_s, dv_s, first_s) = rest[-9:]
    r = pl.program_id(0)
    plen = kv_refs[0].shape[1]
    rlen = q_ref.shape[0]

    @pl.when(r == 0)
    def _():
        for slot in range(prompt_s.shape[0]):
            for j, ref in enumerate(kv_refs):

                @pl.when(sel_ref[slot] == j)
                def _():
                    pltpu.make_async_copy(ref, prompt_s.at[slot], sems.at[slot]).start()

    pltpu.make_async_copy(kv_refs[0], prompt_s.at[r], sems.at[r]).wait()
    k_s[:plen] = prompt_s[r, 0]
    v_s[:plen] = prompt_s[r, 1]
    k_s[plen:] = rk_ref[...]
    v_s[plen:] = rv_ref[...]
    kt_s[...] = k_s[...].T
    vt_s[:HD] = v_s[...].T
    vt_s[HD:] = jnp.ones((ONES, vt_s.shape[1]), BF)
    scale = HD**-0.5
    c = scale * LOG2E
    live = lax.broadcasted_iota(jnp.int32, (1, rlen), 1) < len_ref[r]
    livef = live.astype(F32)
    key_pos = lax.broadcasted_iota(jnp.int32, (rlen, rlen), 0)
    allowed = key_pos <= lax.broadcasted_iota(jnp.int32, (rlen, rlen), 1)
    span = range(heads)
    cols = [pl.ds(h * HD, HD) for h in span]
    scores = [mm(k_s[...], q_ref[:, cols[h]], NT) for h in span]
    grown, rounded = [], []
    for h in span:
        sp = scores[h][:plen]
        sr = jnp.where(allowed, scores[h][plen:], -jnp.inf)
        m = jnp.maximum(jnp.max(sp, axis=0, keepdims=True), jnp.max(sr, axis=0, keepdims=True))
        e = jnp.concatenate([jnp.exp2((sp - m) * c), jnp.exp2((sr - m) * c)], axis=0)
        grown.append(e)
        rounded.append(e.astype(BF))
    outs, douts = [], []
    for h in span:
        both = mm(vt_s[...], rounded[h])
        inv = livef / both[HD : HD + 1]
        ot = both[:HD] * inv
        outs.append(ot)
        o_ref[:, cols[h]] = ot.T.astype(BF)
        douts.append((do_ref[:, cols[h]].T.astype(F32) * inv).astype(BF))
    dss = []
    for h in span:
        delta = jnp.sum(douts[h].astype(F32) * outs[h], axis=0, keepdims=True)
        dss.append((grown[h] * (mm(v_s[...], douts[h]) - delta)).astype(BF))
    for h in span:
        dq_ref[:, cols[h]] = (mm(kt_s[...], dss[h]) * scale).T.astype(BF)
    dv_s[...] = mm(jnp.concatenate(rounded, axis=1), jnp.concatenate(douts, axis=1), NT)
    dk_s[...] = mm(
        jnp.concatenate(dss, axis=1), jnp.concatenate([q_ref[:, cols[h]] for h in span], axis=0)
    )
    rdk_ref[...] = (dk_s[plen:] * scale).astype(BF)
    rdv_ref[...] = dv_s[plen:].astype(BF)

    @pl.when(r == 0)
    def _():
        first_s[0] = dk_s[:plen]
        first_s[1] = dv_s[:plen]

    @pl.when(r == 1)
    def _():
        one, two = sel_ref[0], sel_ref[1]
        for j, part_ref in enumerate(part_refs):

            @pl.when((one != j) & (two != j))
            def _():
                part_ref[...] = jnp.zeros(part_ref.shape, BF)

            @pl.when((one == j) & (two != j))
            def _():
                part_ref[0] = (first_s[0] * scale).astype(BF)
                part_ref[1] = first_s[1].astype(BF)

            @pl.when((one != j) & (two == j))
            def _():
                part_ref[0] = (dk_s[:plen] * scale).astype(BF)
                part_ref[1] = dv_s[:plen].astype(BF)

            @pl.when((one == j) & (two == j))
            def _():
                part_ref[0] = ((first_s[0] + dk_s[:plen]) * scale).astype(BF)
                part_ref[1] = (first_s[1] + dv_s[:plen]).astype(BF)


def attend(g, sel, lengths, q, dout, kvs, rk, rv, prev, loads=()):
    rows, width = q.shape
    slots = sel.shape[0]
    rlen = rows // slots
    gw = width // (rk.shape[1] // HD)
    heads = gw // HD
    plen = kvs[0].shape[1]
    klen = plen + rlen
    wide = pl.BlockSpec((rlen, gw), lambda r, *_: (r, g))
    narrow = pl.BlockSpec((rlen, HD), lambda r, *_: (r, g))
    ins = [q, dout, *kvs, rk, rv]
    in_specs = [wide, wide] + [pl.BlockSpec(memory_space=pltpu.HBM)] * REACH + [narrow, narrow]
    ins += list(loads)
    in_specs += [pl.BlockSpec(memory_space=pltpu.HBM)] * len(loads)
    aliases = {}
    if prev is not None:
        aliases = {2 + len(ins) + i: i for i in range(4)}
        ins += list(prev)
        in_specs += [pl.BlockSpec(memory_space=pl.ANY)] * 4
    return pl.pallas_call(
        functools.partial(attend_kernel, heads, len(loads)),
        out_shape=[jax.ShapeDtypeStruct(q.shape, BF)] * 2
        + [jax.ShapeDtypeStruct(rk.shape, BF)] * 2
        + [jax.ShapeDtypeStruct((2, plen, HD), BF)] * REACH
        + [jax.ShapeDtypeStruct((len(loads), *x.shape), BF) for x in loads[:1]],
        grid_spec=pltpu.PrefetchScalarGridSpec(
            num_scalar_prefetch=2,
            grid=(slots,),
            in_specs=in_specs,
            out_specs=[wide, wide, narrow, narrow]
            + [pl.BlockSpec((2, plen, HD), lambda r, *_: (0, 0, 0))] * REACH
            + [RESIDENT] * bool(loads),
            scratch_shapes=[
                pltpu.VMEM((slots, 2, plen, HD), BF),
                pltpu.SemaphoreType.DMA((slots,)),
            ]
            + [pltpu.VMEM((klen, HD), BF)] * 2
            + [pltpu.VMEM((HD, klen), BF), pltpu.VMEM((HD + ONES, klen), BF)]
            + [pltpu.VMEM((klen, HD), F32)] * 2
            + [pltpu.VMEM((2, plen, HD), F32)]
            + [pltpu.SemaphoreType.DMA((len(loads),))] * bool(loads),
        ),
        input_output_aliases=aliases,
        compiler_params=pltpu.CompilerParams(vmem_limit_bytes=(WHOLE - 6 * MIB) if loads else WHOLE),
        cost_estimate=pl.CostEstimate(
            flops=slots * heads * 24 * rlen * klen * HD,
            bytes_accessed=8 * MIB,
            transcendentals=slots * heads * rlen * klen,
        ),
        name=f"attend_{g}",
    )(sel, lengths, *ins)


def weight_kernel(first, at_ref, both_ref, own_ref, pair_ref, *rest):
    count = at_ref.shape[0]
    arrived, outs = (rest[0], rest[1:]) if rest[0].shape[0] == count and len(rest) > 1 else (None, rest)
    width = outs[0].shape[2]
    own = own_ref[:, first : first + width]
    pair = pair_ref[:, first : first + width]
    each = outs[0].shape[0]
    for i in range(count):
        chunk = at_ref[i]
        total = mm(both_ref[0, chunk], own) + mm(both_ref[1, chunk], pair)
        if arrived is not None:
            total += arrived[i].astype(F32)
        outs[i // each][i % each] = total.astype(BF)


def weight_terms(at, both, grads, columns, arrived=None, parts=1):
    own, pair = grads
    chunk, rows = both.shape[2:]
    count = at.shape[0]
    first, width = columns
    ins = [both, own, pair] + ([] if arrived is None else [arrived])
    return pl.pallas_call(
        functools.partial(weight_kernel, first),
        out_shape=[jax.ShapeDtypeStruct((count // parts, chunk, width), BF)] * parts,
        in_specs=[pl.BlockSpec(memory_space=pltpu.SMEM)] + [RESIDENT] * len(ins),
        out_specs=[RESIDENT] * parts,
        compiler_params=pltpu.CompilerParams(vmem_limit_bytes=SMALL),
        cost_estimate=pl.CostEstimate(
            flops=4 * rows * count * chunk * width,
            bytes_accessed=4 * count * chunk * (rows + width),
            transcendentals=0,
        ),
        name="weight_terms",
    )(at, *ins)


def add(one, two):
    return one.astype(F32) + two.astype(F32)


def hidden_kernel(groups, at_ref, *rest):
    owns, fars, rest = rest[:groups], rest[groups : 2 * groups], rest[2 * groups :]
    (wk_ref, wv_ref, wa_ref, wb_ref, out_ref, grads, weights, done, in_sems, out_sems) = rest
    cols = wa_ref.shape[0]
    steps, tile = weights.shape[1:3]
    copies = []
    for step in range(steps):
        near = pl.ds(pl.multiple_of(at_ref[0] * cols + step * tile, tile), tile)
        away = pl.ds(step * tile, tile)
        sources = (wk_ref.at[near], wv_ref.at[near], wa_ref.at[away], wb_ref.at[away])
        copies.append(
            [
                pltpu.make_async_copy(source, weights.at[j, step], in_sems.at[j, step])
                for j, source in enumerate(sources)
            ]
        )
        for copy in copies[-1]:
            copy.start()
    first = at_ref[1]
    for g in range(groups):
        at = pl.ds(g * HD, HD)
        for j in range(2):
            grads[j, :, at] = owns[g][:, j * HD : (j + 1) * HD]
            away = pl.multiple_of(jnp.where(first == 0, j, 1 - j) * HD, HD)
            grads[2 + j, :, at] = fars[g][:, pl.ds(away, HD)]
    leaving = []
    for step in range(steps):
        for copy in copies[step]:
            copy.wait()
        total = mm(grads[0], weights[0, step], NT)
        for j in range(1, 4):
            total += mm(grads[j], weights[j, step], NT)
        done[step] = total.astype(BF)
        there = out_ref.at[:, pl.ds(step * tile, tile)]
        leaving.append(pltpu.make_async_copy(done.at[step], there, out_sems.at[step]))
        leaving[-1].start()
    for copy in leaving:
        copy.wait()


def hidden_grads(at, owns, fars, w_key, w_value, far_a, far_b):
    groups = len(owns)
    rows = owns[0].shape[0]
    cols, width = far_a.shape
    tile = 512
    steps = cols // tile
    far = pl.BlockSpec(memory_space=pltpu.HBM)
    return pl.pallas_call(
        functools.partial(hidden_kernel, groups),
        out_shape=jax.ShapeDtypeStruct((rows, cols), BF),
        in_specs=[pl.BlockSpec(memory_space=pltpu.SMEM)]
        + [RESIDENT] * (2 * groups)
        + [far] * 4,
        out_specs=far,
        scratch_shapes=[
            pltpu.VMEM((4, rows, width), BF),
            pltpu.VMEM((4, steps, tile, width), BF),
            pltpu.VMEM((steps, rows, tile), BF),
            pltpu.SemaphoreType.DMA((4, steps)),
            pltpu.SemaphoreType.DMA((steps,)),
        ],
        compiler_params=pltpu.CompilerParams(vmem_limit_bytes=VMEM),
        cost_estimate=pl.CostEstimate(
            flops=8 * rows * cols * width,
            bytes_accessed=2 * cols * (rows + 4 * width),
            transcendentals=0,
        ),
        name="hidden_grads",
    )(at, *owns, *fars, w_key, w_value, far_a, far_b)


def total_grad(own, shares):
    total = own.astype(F32)
    for share in shares:
        total += share.astype(F32)
    return jnp.concatenate([total[0], total[1]], axis=-1).astype(BF)


def body(
    prompt_hidden,
    w_key,
    w_value,
    queries,
    resp_key,
    resp_value,
    cotangent,
    group_offset,
    resp_length,
):
    size = lax.axis_size("dp")
    index = lax.axis_index("dp")
    core = index % 2
    half = lax.axis_index("mp")
    groups = w_key.shape[1] // HD
    cols = w_key.shape[0] // 2

    def other(i):
        return (i + 1) % size if i % 2 == 0 else (i + 3) % size

    def back(i):
        return (i - 1) % size if i % 2 == 1 else (i - 3) % size

    def cross(i):
        return (i - 1) % size if i % 2 == 0 else (i - 3) % size

    sel = jnp.where((group_offset % 2 == 1) & (core == 0), 4 - group_offset, group_offset)

    at = jnp.stack([half, core])
    *pairs, near, turned, mine = project(at, prompt_hidden, w_key, w_value, size)
    two = permute(pairs[0], "dp", lambda i: (i + 2) % size, "pair_two")
    one = permute(pairs[0], "dp", other, "pair_other")
    core_two = permute(after(two, sel), "dp", lambda i: i ^ 1, "pair_core")
    received = [[pairs[0], one, two, core_two]]
    far_a = permute(mine, "mp", lambda i: 1 - i, "weights_y")
    far = permute(turned, "dp", lambda i: i ^ 1, "turned_core")
    later = after(pairs[1], two)
    received.append(
        [
            later,
            permute(later, "dp", other, "pair_other"),
            permute(later, "dp", lambda i: (i + 2) % size, "pair_two"),
            permute(later, "dp", lambda i: (i + (1 if i % 2 else 3)) % size, "pair_cross"),
        ]
    )

    *prev, mine_0, other_0, two_0, core_0 = attend(
        0, sel, resp_length, queries, cotangent, received[0], resp_key, resp_value, None
    )
    shares = [
        permute(other_0, "dp", back, "grad_other"),
        permute(two_0, "dp", lambda i: (i - 2) % size, "grad_two"),
        permute(core_0, "dp", cross, "grad_cross"),
    ]
    received[1], far, far_a, prev = after((received[1], far, far_a, prev), mine_0)
    *prev, mine_1, other_1, two_1, core_1, both = attend(
        1,
        sel,
        resp_length,
        queries,
        cotangent,
        received[1],
        resp_key,
        resp_value,
        prev,
        (near, far),
    )
    far_b = permute(far_a, "dp", lambda i: i ^ 1, "weights_core")
    swapped = permute(core_1, "dp", lambda i: i ^ 1, "grad_core")
    shares_1 = [permute(other_1, "dp", back, "grad_other")]

    own = [total_grad(after(mine_0, mine_1), shares)]
    pair = [permute(own[0], "dp", lambda i: i ^ 1, "own_core")]
    two = after((two_1.astype(F32) + swapped.astype(F32)).astype(BF), own[0])
    shares_1.append(permute(two, "dp", lambda i: (i - 2) % size, "grad_two"))

    bit, place = (index // 2) % 2, index // 4
    count = both.shape[1]

    def places(shifts, flips):
        return jnp.stack([2 * (place ^ i) + (bit ^ x) for i in shifts for x in flips])

    def along(block, bits, name):
        return permute(block, "dp", lambda i: i ^ bits, name)

    def far_sum(kept, rest, bits):
        while rest:
            sent = jnp.stack([rest[0]] + rest[1:][1::2])
            got = along(sent.astype(BF), bits, "terms_z")
            kept = add(kept, got[0])
            rest = [add(r, g) for r, g in zip(rest[1:][0::2], got[1:])]
            bits *= 2
        return kept

    whole = (0, 2 * HD)
    every = range(count // 2)
    if count // 2 != REACH:
        owns = own + [total_grad(mine_1, shares_1)]
        weight_grads = []
        for grad in owns:
            grads = (grad, permute(grad, "dp", lambda i: i ^ 1, "own_core"))
            (sent,) = weight_terms(places(every, [1]), both, grads, whole)
            got = along(sent, 2, "terms_x")
            (held,) = weight_terms(places(every, [0]), both, grads, whole, got)
            weight_grads.append(far_sum(held[0], list(held[1:]), 4))
        away = [permute(grad, "mp", lambda i: 1 - i, "own_y") for grad in owns]
        hidden_grad = hidden_grads(at, owns, away, w_key, w_value, far_a, far_b)
        keys = [t[:, :HD] for t in weight_grads]
        values = [t[:, HD:] for t in weight_grads]
        return (
            *prev,
            hidden_grad,
            jnp.concatenate(keys, axis=-1),
            jnp.concatenate(values, axis=-1),
        )

    key, value = (0, HD), (HD, HD)
    near_first, near_then = [0, 2], [1, 3]
    every = near_first + near_then
    grads_0 = (after(own[0], two), pair[0])
    (sent_0,) = weight_terms(places(every, [1]), both, grads_0, whole)
    got_0 = along(sent_0, 2, "terms_x")
    away = [permute(after(own[0], sent_0), "mp", lambda i: 1 - i, "own_y")]
    own.append(total_grad(after(mine_1, sent_0), shares_1))
    pair.append(permute(own[1], "dp", lambda i: i ^ 1, "own_core"))
    grads_1 = (own[1], pair[1])
    (sent_v,) = weight_terms(places([1, 3], [0, 1]), both, grads_1, value)
    got_v = along(sent_v, 4, "terms_z1")
    (sent_k,) = weight_terms(places(every, [1]), both, (after(own[1], sent_v), pair[1]), key)
    got_k = along(sent_k, 2, "terms_x")

    held_0, sent_0 = weight_terms(
        places(every, [0]), both, grads_0, whole,
        after(got_0, sent_k, away[0]), 2,
    )
    got_0 = along(sent_0, 4, "terms_z1")
    away.append(permute(after(own[1], held_0), "mp", lambda i: 1 - i, "own_y"))
    held_v, sent_v = weight_terms(
        places(near_first, [0, 1]), both, grads_1, value, after(got_v, held_0), 2
    )
    got_v = along(sent_v, 8, "terms_z2")
    held_k, sent_k = weight_terms(
        places(every, [0]), both, grads_1, key, after(got_k, held_v, away[1]), 2
    )
    got_k = along(sent_k, 4, "terms_z1")
    two_v = add(held_v[1], after(got_v, held_k)[1]).astype(BF)
    last_v = along(two_v, 2, "terms_x")
    two_0 = add(held_0[1], after(got_0, two_v)[1]).astype(BF)
    last_0 = along(two_0, 8, "terms_z2")
    two_k = add(held_k[1], after(got_k, two_0)[1]).astype(BF)
    last_k = along(two_k, 8, "terms_z2")
    hidden_grad = hidden_grads(
        at, after(own, two_0, two_v, two_k), away, w_key, w_value, far_a, far_b
    )
    last_0, last_v, last_k = after((last_0, last_v, last_k), hidden_grad)
    total_0 = add(add(held_0[0], got_0[0]), last_0)
    total_v = add(add(held_v[0], got_v[0]), last_v)
    total_k = add(add(held_k[0], got_k[0]), last_k)
    return (
        *prev,
        hidden_grad,
        jnp.concatenate([total_0[:, :HD], total_k], axis=-1),
        jnp.concatenate([total_0[:, HD:], total_v], axis=-1),
    )


def solution(mesh):
    placed = (
        P("dp", None),
        P(None, "mp"),
        P(None, "mp"),
        P("dp", "mp"),
        P("dp", "mp"),
        P("dp", "mp"),
        P("dp", "mp"),
        P("dp"),
        P("dp"),
    )
    return jax.shard_map(
        body,
        mesh=mesh,
        in_specs=placed,
        out_specs=(P("dp", "mp"),) * 7,
        check_vma=False,
    )
```

```python
import functools
import math

import jax
import jax.numpy as jnp
from jax import lax
from jax.experimental import pallas as pl
from jax.experimental.pallas import tpu as pltpu
from jax.sharding import PartitionSpec as P

HD = 128
REACH = 4
ONES = 16
LOG2E = 1.4426950408889634
BF = jnp.bfloat16
F32 = jnp.float32
NT = (((1,), (1,)), ((), ()))
NN = (((1,), (0,)), ((), ()))
TN = (((0,), (0,)), ((), ()))
MIB = 1024 * 1024
VMEM = 16 * MIB
SMALL = 12 * MIB
WHOLE = 58 * MIB
ATTEND = 36 * MIB
RESIDENT = pl.BlockSpec(memory_space=pltpu.VMEM)


def mm(a, b, dims=NN):
    return lax.dot_general(a, b, dims, preferred_element_type=F32)


def permute(block, axis, target, name):
    with jax.named_scope(name):
        return lax.ppermute(block, axis, [(i, target(i)) for i in range(lax.axis_size(axis))])


def after(values, *others):
    return lax.optimization_barrier((values, others))[0]


def project_kernel(groups, at_ref, h_ref, wk_ref, wv_ref, *rest):
    outs, (keep_ref, send_ref, mine_ref), rest = rest[:groups], rest[groups : groups + 3], rest[groups + 3 :]
    h_s, wk_s, wv_s, turned, in_sems, out_sems, mine_sems = rest
    steps, rows, tile = h_s.shape
    width = wk_s.shape[2]
    chunk = keep_ref.shape[1]
    pairs = tile // (2 * chunk)
    half, core = at_ref[0], at_ref[1]
    copies = []
    for j in range(steps):
        at = pl.ds(j * tile, tile)
        copies.append(
            [
                pltpu.make_async_copy(h_ref.at[:, at], h_s.at[j], in_sems.at[j, 0]),
                pltpu.make_async_copy(wk_ref.at[at], wk_s.at[j], in_sems.at[j, 1]),
                pltpu.make_async_copy(wv_ref.at[at], wv_s.at[j], in_sems.at[j, 2]),
            ]
        )
        for copy in copies[-1]:
            copy.start()
    key = value = jnp.zeros((rows, width), F32)
    leaving = []
    for j in range(steps):
        for copy in copies[j]:
            copy.wait()
        key += mm(h_s[j], wk_s[j])
        value += mm(h_s[j], wv_s[j])
        turned[j] = h_s[j].T
        for p in range(pairs):
            for which, out in ((core, keep_ref), (1 - core, send_ref)):
                at = pl.ds(pl.multiple_of((2 * p + which) * chunk, chunk), chunk)
                there = out.at[j * pairs + p]
                sem = out_sems.at[j, p, 0 if out is keep_ref else 1]
                leaving.append(pltpu.make_async_copy(turned.at[j, at], there, sem))
                leaving[-1].start()
    for j in range(steps // 2):
        there = mine_ref.at[pl.ds(j * tile, tile)]
        away = (1 - half) * (steps // 2) + j

        @pl.when(core == 0)
        def _():
            pltpu.make_async_copy(wk_s.at[away], there, mine_sems.at[j]).start()

        @pl.when(core != 0)
        def _():
            pltpu.make_async_copy(wv_s.at[away], there, mine_sems.at[j]).start()

        leaving.append(pltpu.make_async_copy(wk_s.at[away], there, mine_sems.at[j]))
    for g, out in enumerate(outs):
        out[0] = key[:, g * HD : (g + 1) * HD].astype(BF)
        out[1] = value[:, g * HD : (g + 1) * HD].astype(BF)
    for copy in leaving:
        copy.wait()


def project(at, hidden, w_key, w_value, parts):
    rows, depth = hidden.shape
    width = w_key.shape[1]
    steps = 4
    tile = depth // steps
    chunk = depth // parts
    groups = width // HD
    far = pl.BlockSpec(memory_space=pltpu.HBM)
    turned = jax.ShapeDtypeStruct((parts // 2, chunk, rows), BF)
    return pl.pallas_call(
        functools.partial(project_kernel, groups),
        out_shape=[jax.ShapeDtypeStruct((2, rows, HD), BF)] * groups
        + [turned, turned, jax.ShapeDtypeStruct((depth // 2, width), BF)],
        in_specs=[pl.BlockSpec(memory_space=pltpu.SMEM)] + [far] * 3,
        out_specs=[RESIDENT] * groups + [far] * 3,
        scratch_shapes=[
            pltpu.VMEM((steps, rows, tile), BF),
            pltpu.VMEM((steps, tile, width), BF),
            pltpu.VMEM((steps, tile, width), BF),
            pltpu.VMEM((steps, tile, rows), BF),
            pltpu.SemaphoreType.DMA((steps, 3)),
            pltpu.SemaphoreType.DMA((steps, tile // (2 * chunk), 2)),
            pltpu.SemaphoreType.DMA((steps // 2,)),
        ],
        compiler_params=pltpu.CompilerParams(vmem_limit_bytes=WHOLE),
        cost_estimate=pl.CostEstimate(
            flops=4 * rows * depth * width,
            bytes_accessed=4 * depth * (rows + width),
            transcendentals=0,
        ),
        name="project",
    )(at, hidden, w_key, w_value)


def attend_kernel(heads, loads, sel_ref, len_ref, q_ref, do_ref, *rest):
    if loads:
        sources, landed = rest[REACH + 2 : REACH + 2 + loads], rest[-10 - loads : -10]
        load_sems = rest[-1]
        rest = rest[: REACH + 2] + rest[REACH + 2 + loads : -10 - loads] + rest[-10:-1]
        moves = [
            pltpu.make_async_copy(src, dst, load_sems.at[i])
            for i, (src, dst) in enumerate(zip(sources, landed))
        ]

        @pl.when(pl.program_id(0) == 0)
        def _():
            for move in moves:
                move.start()

        @pl.when(pl.program_id(0) == pl.num_programs(0) - 1)
        def _():
            for move in moves:
                move.wait()

    kv_refs, (rk_ref, rv_ref), rest = rest[:REACH], rest[REACH : REACH + 2], rest[REACH + 2 :]
    (o_ref, dq_ref, rdk_ref, rdv_ref, *part_refs) = rest[-13 - REACH : -9]
    (prompt_s, sems, k_s, v_s, kt_s, vt_s, dk_s, dv_s, first_s) = rest[-9:]
    r = pl.program_id(0)
    plen = kv_refs[0].shape[1]
    rlen = q_ref.shape[0]

    @pl.when(r == 0)
    def _():
        for slot in range(prompt_s.shape[0]):
            for j, ref in enumerate(kv_refs):

                @pl.when(sel_ref[slot] == j)
                def _():
                    pltpu.make_async_copy(ref, prompt_s.at[slot], sems.at[slot]).start()

    pltpu.make_async_copy(kv_refs[0], prompt_s.at[r], sems.at[r]).wait()
    k_s[:plen] = prompt_s[r, 0]
    v_s[:plen] = prompt_s[r, 1]
    k_s[plen:] = rk_ref[...]
    v_s[plen:] = rv_ref[...]
    kt_s[...] = k_s[...].T
    vt_s[:HD] = v_s[...].T
    vt_s[HD:] = jnp.ones((ONES, vt_s.shape[1]), BF)
    scale = HD**-0.5
    c = scale * LOG2E
    live = lax.broadcasted_iota(jnp.int32, (1, rlen), 1) < len_ref[r]
    livef = live.astype(F32)
    key_pos = lax.broadcasted_iota(jnp.int32, (rlen, rlen), 0)
    allowed = key_pos <= lax.broadcasted_iota(jnp.int32, (rlen, rlen), 1)
    span = range(heads)
    cols = [pl.ds(h * HD, HD) for h in span]
    scores = [mm(k_s[...], q_ref[:, cols[h]], NT) for h in span]
    grown, rounded = [], []
    for h in span:
        sp = scores[h][:plen]
        sr = jnp.where(allowed, scores[h][plen:], -jnp.inf)
        m = jnp.maximum(jnp.max(sp, axis=0, keepdims=True), jnp.max(sr, axis=0, keepdims=True))
        e = jnp.concatenate([jnp.exp2((sp - m) * c), jnp.exp2((sr - m) * c)], axis=0)
        grown.append(e)
        rounded.append(e.astype(BF))
    outs, douts = [], []
    for h in span:
        both = mm(vt_s[...], rounded[h])
        inv = livef / both[HD : HD + 1]
        ot = both[:HD] * inv
        outs.append(ot)
        o_ref[:, cols[h]] = ot.T.astype(BF)
        douts.append((do_ref[:, cols[h]].T.astype(F32) * inv).astype(BF))
    dss = []
    for h in span:
        delta = jnp.sum(douts[h].astype(F32) * outs[h], axis=0, keepdims=True)
        dss.append((grown[h] * (mm(v_s[...], douts[h]) - delta)).astype(BF))
    for h in span:
        dq_ref[:, cols[h]] = (mm(kt_s[...], dss[h]) * scale).T.astype(BF)
    dv_s[...] = mm(jnp.concatenate(rounded, axis=1), jnp.concatenate(douts, axis=1), NT)
    dk_s[...] = mm(
        jnp.concatenate(dss, axis=1), jnp.concatenate([q_ref[:, cols[h]] for h in span], axis=0)
    )
    rdk_ref[...] = (dk_s[plen:] * scale).astype(BF)
    rdv_ref[...] = dv_s[plen:].astype(BF)

    @pl.when(r == 0)
    def _():
        first_s[0] = dk_s[:plen]
        first_s[1] = dv_s[:plen]

    @pl.when(r == 1)
    def _():
        one, two = sel_ref[0], sel_ref[1]
        for j, part_ref in enumerate(part_refs):

            @pl.when((one != j) & (two != j))
            def _():
                part_ref[...] = jnp.zeros(part_ref.shape, BF)

            @pl.when((one == j) & (two != j))
            def _():
                part_ref[0] = (first_s[0] * scale).astype(BF)
                part_ref[1] = first_s[1].astype(BF)

            @pl.when((one != j) & (two == j))
            def _():
                part_ref[0] = (dk_s[:plen] * scale).astype(BF)
                part_ref[1] = dv_s[:plen].astype(BF)

            @pl.when((one == j) & (two == j))
            def _():
                part_ref[0] = ((first_s[0] + dk_s[:plen]) * scale).astype(BF)
                part_ref[1] = (first_s[1] + dv_s[:plen]).astype(BF)


def attend(g, sel, lengths, q, dout, kvs, rk, rv, prev, loads=()):
    rows, width = q.shape
    slots = sel.shape[0]
    rlen = rows // slots
    gw = width // (rk.shape[1] // HD)
    heads = gw // HD
    plen = kvs[0].shape[1]
    klen = plen + rlen
    wide = pl.BlockSpec((rlen, gw), lambda r, *_: (r, g))
    narrow = pl.BlockSpec((rlen, HD), lambda r, *_: (r, g))
    ins = [q, dout, *kvs, rk, rv]
    in_specs = [wide, wide] + [pl.BlockSpec(memory_space=pltpu.HBM)] * REACH + [narrow, narrow]
    ins += list(loads)
    in_specs += [pl.BlockSpec(memory_space=pltpu.HBM)] * len(loads)
    aliases = {}
    if prev is not None:
        aliases = {2 + len(ins) + i: i for i in range(4)}
        ins += list(prev)
        in_specs += [pl.BlockSpec(memory_space=pl.ANY)] * 4
    return pl.pallas_call(
        functools.partial(attend_kernel, heads, len(loads)),
        out_shape=[jax.ShapeDtypeStruct(q.shape, BF)] * 2
        + [jax.ShapeDtypeStruct(rk.shape, BF)] * 2
        + [jax.ShapeDtypeStruct((2, plen, HD), BF)] * REACH
        + [jax.ShapeDtypeStruct(x.shape, x.dtype) for x in loads],
        grid_spec=pltpu.PrefetchScalarGridSpec(
            num_scalar_prefetch=2,
            grid=(slots,),
            in_specs=in_specs,
            out_specs=[wide, wide, narrow, narrow]
            + [pl.BlockSpec((2, plen, HD), lambda r, *_: (0, 0, 0))] * REACH
            + [RESIDENT] * len(loads),
            scratch_shapes=[
                pltpu.VMEM((slots, 2, plen, HD), BF),
                pltpu.SemaphoreType.DMA((slots,)),
            ]
            + [pltpu.VMEM((klen, HD), BF)] * 2
            + [pltpu.VMEM((HD, klen), BF), pltpu.VMEM((HD + ONES, klen), BF)]
            + [pltpu.VMEM((klen, HD), F32)] * 2
            + [pltpu.VMEM((2, plen, HD), F32)]
            + [pltpu.SemaphoreType.DMA((len(loads),))] * bool(loads),
        ),
        input_output_aliases=aliases,
        compiler_params=pltpu.CompilerParams(vmem_limit_bytes=ATTEND),
        cost_estimate=pl.CostEstimate(
            flops=slots * heads * 24 * rlen * klen * HD,
            bytes_accessed=8 * MIB,
            transcendentals=slots * heads * rlen * klen,
        ),
        name=f"attend_{g}",
    )(sel, lengths, *ins)


def weight_kernel(first, at_ref, near_ref, far_ref, own_ref, pair_ref, *rest):
    count = at_ref.shape[0]
    arrived, outs = (rest[0], rest[1:]) if rest[0].shape[0] == count and len(rest) > 1 else (None, rest)
    width = outs[0].shape[2]
    own = own_ref[:, first : first + width]
    pair = pair_ref[:, first : first + width]
    each = outs[0].shape[0]
    for i in range(count):
        chunk = at_ref[i]
        total = mm(near_ref[chunk], own) + mm(far_ref[chunk], pair)
        if arrived is not None:
            total += arrived[i].astype(F32)
        outs[i // each][i % each] = total.astype(BF)


def weight_terms(at, near, far, grads, columns, arrived=None, parts=1):
    own, pair = grads
    chunk, rows = near.shape[1:]
    count = at.shape[0]
    first, width = columns
    ins = [near, far, own, pair] + ([] if arrived is None else [arrived])
    return pl.pallas_call(
        functools.partial(weight_kernel, first),
        out_shape=[jax.ShapeDtypeStruct((count // parts, chunk, width), BF)] * parts,
        in_specs=[pl.BlockSpec(memory_space=pltpu.SMEM)] + [RESIDENT] * len(ins),
        out_specs=[RESIDENT] * parts,
        compiler_params=pltpu.CompilerParams(vmem_limit_bytes=SMALL),
        cost_estimate=pl.CostEstimate(
            flops=4 * rows * count * chunk * width,
            bytes_accessed=4 * count * chunk * (rows + width),
            transcendentals=0,
        ),
        name="weight_terms",
    )(at, *ins)


def add(one, two):
    return one.astype(F32) + two.astype(F32)


def hidden_kernel(groups, at_ref, *rest):
    owns, fars, rest = rest[:groups], rest[groups : 2 * groups], rest[2 * groups :]
    (wk_ref, wv_ref, wa_ref, wb_ref, out_ref, grads, weights, done, in_sems, out_sems) = rest
    cols = wa_ref.shape[0]
    steps, tile = weights.shape[1:3]
    copies = []
    for step in range(steps):
        near = pl.ds(pl.multiple_of(at_ref[0] * cols + step * tile, tile), tile)
        away = pl.ds(step * tile, tile)
        sources = (wk_ref.at[near], wv_ref.at[near], wa_ref.at[away], wb_ref.at[away])
        copies.append(
            [
                pltpu.make_async_copy(source, weights.at[j, step], in_sems.at[j, step])
                for j, source in enumerate(sources)
            ]
        )
        for copy in copies[-1]:
            copy.start()
    first = at_ref[1]
    for g in range(groups):
        at = pl.ds(g * HD, HD)
        for j in range(2):
            grads[j, :, at] = owns[g][:, j * HD : (j + 1) * HD]
            away = pl.multiple_of(jnp.where(first == 0, j, 1 - j) * HD, HD)
            grads[2 + j, :, at] = fars[g][:, pl.ds(away, HD)]
    leaving = []
    for step in range(steps):
        for copy in copies[step]:
            copy.wait()
        total = mm(grads[0], weights[0, step], NT)
        for j in range(1, 4):
            total += mm(grads[j], weights[j, step], NT)
        done[step] = total.astype(BF)
        there = out_ref.at[:, pl.ds(step * tile, tile)]
        leaving.append(pltpu.make_async_copy(done.at[step], there, out_sems.at[step]))
        leaving[-1].start()
    for copy in leaving:
        copy.wait()


def hidden_grads(at, owns, fars, w_key, w_value, far_a, far_b):
    groups = len(owns)
    rows = owns[0].shape[0]
    cols, width = far_a.shape
    tile = 512
    steps = cols // tile
    far = pl.BlockSpec(memory_space=pltpu.HBM)
    return pl.pallas_call(
        functools.partial(hidden_kernel, groups),
        out_shape=jax.ShapeDtypeStruct((rows, cols), BF),
        in_specs=[pl.BlockSpec(memory_space=pltpu.SMEM)]
        + [RESIDENT] * (2 * groups)
        + [far] * 4,
        out_specs=far,
        scratch_shapes=[
            pltpu.VMEM((4, rows, width), BF),
            pltpu.VMEM((4, steps, tile, width), BF),
            pltpu.VMEM((steps, rows, tile), BF),
            pltpu.SemaphoreType.DMA((4, steps)),
            pltpu.SemaphoreType.DMA((steps,)),
        ],
        compiler_params=pltpu.CompilerParams(vmem_limit_bytes=VMEM),
        cost_estimate=pl.CostEstimate(
            flops=8 * rows * cols * width,
            bytes_accessed=2 * cols * (rows + 4 * width),
            transcendentals=0,
        ),
        name="hidden_grads",
    )(at, *owns, *fars, w_key, w_value, far_a, far_b)


def total_grad(own, shares):
    total = own.astype(F32)
    for share in shares:
        total += share.astype(F32)
    return jnp.concatenate([total[0], total[1]], axis=-1).astype(BF)


def body(
    prompt_hidden,
    w_key,
    w_value,
    queries,
    resp_key,
    resp_value,
    cotangent,
    group_offset,
    resp_length,
):
    size = lax.axis_size("dp")
    index = lax.axis_index("dp")
    core = index % 2
    half = lax.axis_index("mp")
    groups = w_key.shape[1] // HD
    cols = w_key.shape[0] // 2

    def other(i):
        return (i + 1) % size if i % 2 == 0 else (i + 3) % size

    def back(i):
        return (i - 1) % size if i % 2 == 1 else (i - 3) % size

    def cross(i):
        return (i - 1) % size if i % 2 == 0 else (i - 3) % size

    sel = jnp.where((group_offset % 2 == 1) & (core == 0), 4 - group_offset, group_offset)

    at = jnp.stack([half, core])
    *pairs, near, turned, mine = project(at, prompt_hidden, w_key, w_value, size)
    two = permute(pairs[0], "dp", lambda i: (i + 2) % size, "pair_two")
    one = permute(pairs[0], "dp", other, "pair_other")
    core_two = permute(after(two, sel), "dp", lambda i: i ^ 1, "pair_core")
    received = [[pairs[0], one, two, core_two]]
    far_a = permute(mine, "mp", lambda i: 1 - i, "weights_y")
    far = permute(turned, "dp", lambda i: i ^ 1, "turned_core")
    later = after(pairs[1], two)
    received.append(
        [
            later,
            permute(later, "dp", other, "pair_other"),
            permute(later, "dp", lambda i: (i + 2) % size, "pair_two"),
            permute(later, "dp", lambda i: (i + (1 if i % 2 else 3)) % size, "pair_cross"),
        ]
    )

    *prev, mine_0, other_0, two_0, core_0 = attend(
        0, sel, resp_length, queries, cotangent, received[0], resp_key, resp_value, None
    )
    shares = [
        permute(other_0, "dp", back, "grad_other"),
        permute(two_0, "dp", lambda i: (i - 2) % size, "grad_two"),
        permute(core_0, "dp", cross, "grad_cross"),
    ]
    received[1], far, far_a, prev = after((received[1], far, far_a, prev), mine_0)
    *prev, mine_1, other_1, two_1, core_1, near, far = attend(
        1,
        sel,
        resp_length,
        queries,
        cotangent,
        received[1],
        resp_key,
        resp_value,
        prev,
        (near, far),
    )
    far_b = permute(far_a, "dp", lambda i: i ^ 1, "weights_core")
    swapped = permute(core_1, "dp", lambda i: i ^ 1, "grad_core")
    shares_1 = [permute(other_1, "dp", back, "grad_other")]

    own = [total_grad(after(mine_0, mine_1), shares)]
    pair = [permute(own[0], "dp", lambda i: i ^ 1, "own_core")]
    two = after((two_1.astype(F32) + swapped.astype(F32)).astype(BF), own[0])
    shares_1.append(permute(two, "dp", lambda i: (i - 2) % size, "grad_two"))

    bit, place = (index // 2) % 2, index // 4
    count = near.shape[0]

    def places(shifts, flips):
        return jnp.stack([2 * (place ^ i) + (bit ^ x) for i in shifts for x in flips])

    def along(block, bits, name):
        return permute(block, "dp", lambda i: i ^ bits, name)

    def far_sum(kept, rest, bits):
        while rest:
            sent = jnp.stack([rest[0]] + rest[1:][1::2])
            got = along(sent.astype(BF), bits, "terms_z")
            kept = add(kept, got[0])
            rest = [add(r, g) for r, g in zip(rest[1:][0::2], got[1:])]
            bits *= 2
        return kept

    whole = (0, 2 * HD)
    every = range(count // 2)
    if count // 2 != REACH:
        owns = own + [total_grad(mine_1, shares_1)]
        weight_grads = []
        for grad in owns:
            grads = (grad, permute(grad, "dp", lambda i: i ^ 1, "own_core"))
            (sent,) = weight_terms(places(every, [1]), near, far, grads, whole)
            got = along(sent, 2, "terms_x")
            (held,) = weight_terms(places(every, [0]), near, far, grads, whole, got)
            weight_grads.append(far_sum(held[0], list(held[1:]), 4))
        away = [permute(grad, "mp", lambda i: 1 - i, "own_y") for grad in owns]
        hidden_grad = hidden_grads(at, owns, away, w_key, w_value, far_a, far_b)
        keys = [t[:, :HD] for t in weight_grads]
        values = [t[:, HD:] for t in weight_grads]
        return (
            *prev,
            hidden_grad,
            jnp.concatenate(keys, axis=-1),
            jnp.concatenate(values, axis=-1),
        )

    key, value = (0, HD), (HD, HD)
    near_first, near_then = [0, 2], [1, 3]
    every = near_first + near_then
    grads_0 = (after(own[0], two), pair[0])
    (sent_0,) = weight_terms(places(every, [1]), near, far, grads_0, whole)
    got_0 = along(sent_0, 2, "terms_x")
    away = [permute(after(own[0], sent_0), "mp", lambda i: 1 - i, "own_y")]
    own.append(total_grad(after(mine_1, sent_0, away[0]), shares_1))
    pair.append(permute(own[1], "dp", lambda i: i ^ 1, "own_core"))
    grads_1 = (own[1], pair[1])
    (sent_v,) = weight_terms(places([1, 3], [0, 1]), near, far, grads_1, value)
    got_v = along(sent_v, 4, "terms_z1")
    (sent_k,) = weight_terms(places(every, [1]), near, far, (after(own[1], sent_v), pair[1]), key)
    got_k = along(sent_k, 2, "terms_x")

    held_0, sent_0 = weight_terms(
        places(every, [0]), near, far, grads_0, whole,
        after(got_0, sent_k), 2,
    )
    got_0 = along(sent_0, 4, "terms_z1")
    away.append(permute(after(own[1], held_0), "mp", lambda i: 1 - i, "own_y"))
    held_v, sent_v = weight_terms(
        places(near_first, [0, 1]), near, far, grads_1, value, after(got_v, held_0), 2
    )
    got_v = along(sent_v, 8, "terms_z2")
    held_k, sent_k = weight_terms(
        places(every, [0]), near, far, grads_1, key, after(got_k, held_v, away[1]), 2
    )
    got_k = along(sent_k, 4, "terms_z1")
    two_0 = add(held_0[1], after(got_0, held_k)[1]).astype(BF)
    last_0 = along(two_0, 8, "terms_z2")
    two_v = add(held_v[1], after(got_v, two_0)[1]).astype(BF)
    last_v = along(two_v, 2, "terms_x")
    two_k = add(held_k[1], after(got_k, two_v)[1]).astype(BF)
    last_k = along(two_k, 8, "terms_z2")
    hidden_grad = hidden_grads(
        at, after(own, two_0, two_v, two_k), away, w_key, w_value, far_a, far_b
    )
    last_0, last_v, last_k = after((last_0, last_v, last_k), hidden_grad)
    total_0 = add(add(held_0[0], got_0[0]), last_0)
    total_v = add(add(held_v[0], got_v[0]), last_v)
    total_k = add(add(held_k[0], got_k[0]), last_k)
    return (
        *prev,
        hidden_grad,
        jnp.concatenate([total_0[:, :HD], total_k], axis=-1),
        jnp.concatenate([total_0[:, HD:], total_v], axis=-1),
    )


def solution(mesh):
    placed = (
        P("dp", None),
        P(None, "mp"),
        P(None, "mp"),
        P("dp", "mp"),
        P("dp", "mp"),
        P("dp", "mp"),
        P("dp", "mp"),
        P("dp"),
        P("dp"),
    )
    return jax.shard_map(
        body,
        mesh=mesh,
        in_specs=placed,
        out_specs=(P("dp", "mp"),) * 7,
        check_vma=False,
    )
```
